32 devices in a mesh: index: 4 (over y, core), bulk: 8 (over z, x).
Axes of the slice: x: 2, y: 2, z: 4, core: 2. Of those that a mesh axis runs over, the one named last changes fastest.
Arguments:
- questions: bfloat16 [1024, 768], P(('index', 'bulk')), may hold values from -26 to 26
- passages: bfloat16 [65536, 768], P(('index', 'bulk')), may hold values from -6 to 6
- candidate_ids: int32 [1024, 32], P(('index', 'bulk')), may hold values from 0 to 65535, as said below
- reader_loglik: float32 [1024, 32], P(('index', 'bulk')), may hold values from -400 to 0
Outputs:
- mean_divergence: float32 [], replicated
- question_grads: float32 [1024, 768], P(('index', 'bulk'))
The draws below stay inside these ranges and needn't reach their ends.
Inputs may be any that keep to these rules, and one draw needn't show every extreme that they name: `candidate_ids`: passage id p lies in the range of owner p // 2048. Among the 32 candidates of the 32 questions of one device, at most 64 lie in one owner's range; in every draw some owner has exactly 64 from every device, and every owner has at least one from every device.
All inputs are finite; a program needn't handle non-finite values.
Results may differ from the reference program's by a relative error of at most 0.0024.
Values may be sent and summed in bfloat16 or wider, within the bound.
A program may use at most 64 MiB of HBM per device.

```python
import math
import jax
import jax.numpy as jnp
from jax import lax

D = 768
P_DEV = 2048
Q_DEV = 32
K = 32
OWNERS = 32
CAP = 64
QUESTIONS = 1024
PASSAGES = 65536


def passage_rows(key, row_ids):
    base_key = jax.random.fold_in(key, 202)

    def one_row(row_id):
        row_key = jax.random.fold_in(base_key, row_id)
        return jnp.clip(jax.random.normal(row_key, (D,), jnp.float32), -6.0, 6.0)
    return jax.vmap(one_row)(row_ids)


def permute_slots(sub_key):
    return jax.random.permutation(sub_key, OWNERS * CAP)


def permute_pairs(sub_key):
    return jax.random.permutation(sub_key, Q_DEV * K)


def route_plan(key):
    base_key = jax.random.fold_in(key, 303)
    key_list = jax.random.split(base_key, 6)
    popular = jax.random.randint(key_list[0], (OWNERS,), 1, 9)
    weight = popular[None, :] + jax.random.randint(key_list[1], (OWNERS, OWNERS), 0, 3)
    hottest = jax.random.randint(key_list[2], (), 0, OWNERS)
    weight = jnp.where(jnp.arange(OWNERS)[None, :] == hottest, 0, weight)
    slot_rank = jnp.arange(CAP)
    order_key = (slot_rank[None, None, :] * weight[:, :, None]).reshape(OWNERS, OWNERS * CAP)
    tie_break = jax.vmap(permute_slots)(jax.random.split(key_list[3], OWNERS))
    ordered = order_key * (OWNERS * CAP) + tie_break
    chosen = jnp.argsort(ordered, axis=1)[:, :Q_DEV * K]
    shuffle = jax.vmap(permute_pairs)(jax.random.split(key_list[4], OWNERS))
    chosen = jnp.take_along_axis(chosen, shuffle, axis=1)
    owner_of = chosen // CAP
    row_of = jax.random.randint(key_list[5], (OWNERS, Q_DEV * K), 0, P_DEV)
    columns = jnp.arange(Q_DEV * K)[None, :]
    low_place = jnp.argmax((owner_of == 0).astype(jnp.int32), axis=1)
    high_place = jnp.argmax((owner_of == OWNERS - 1).astype(jnp.int32), axis=1)
    row_of = jnp.where(columns == low_place[:, None], 0, row_of)
    row_of = jnp.where(columns == high_place[:, None], P_DEV - 1, row_of)
    return (owner_of * P_DEV + row_of).reshape(QUESTIONS, K).astype(jnp.int32)


def draw_candidate_ids(key, part):
    return route_plan(key)


def draw_passages(key, part):
    return passage_rows(key, jnp.arange(PASSAGES, dtype=jnp.int32)).astype(jnp.bfloat16)


def draw_questions(key, part):
    position = jnp.arange(QUESTIONS).astype(jnp.float32) / max(QUESTIONS - 1, 1)
    key_list = jax.random.split(jax.random.fold_in(key, 404), 1)
    row_scale = 1.0 + 2.0 * position
    return (jnp.clip(jax.random.normal(key_list[0], (QUESTIONS, D), jnp.float32), -6.0, 6.0) * row_scale[:, None]).astype(jnp.bfloat16)


def draw_reader_loglik(key, part):
    position = jnp.arange(QUESTIONS).astype(jnp.float32) / max(QUESTIONS - 1, 1)
    key_list = jax.random.split(jax.random.fold_in(key, 505), 1)
    spread = jax.random.uniform(key_list[0], (QUESTIONS, K), jnp.float32, 0.0, 3.0)
    row_scale = 1.0 + 3.0 * position
    return -row_scale[:, None] * spread


def setup_inputs(seed: int = 0) -> dict:
    keys = jax.random.split(jax.random.key(seed), 5)
    questions = draw_questions(jax.random.fold_in(keys[4], 71), 0)
    passages = draw_passages(jax.random.fold_in(keys[4], 71), 0)
    candidate_ids = draw_candidate_ids(jax.random.fold_in(keys[4], 71), 0)
    reader_loglik = draw_reader_loglik(jax.random.fold_in(keys[4], 71), 0)
    return {"questions": questions, "passages": passages, "candidate_ids": candidate_ids, "reader_loglik": reader_loglik}


def log_normalize(logits):
    highest = lax.optimization_barrier(jnp.max(logits, axis=1, keepdims=True))
    shifted = logits - highest
    return shifted - jnp.log(lax.optimization_barrier(jnp.sum(jnp.exp(shifted), axis=1, keepdims=True)))

def reference(questions, passages, candidate_ids, reader_loglik):
    block_rows = math.gcd(QUESTIONS, 512)
    blocks = QUESTIONS // block_rows
    score_scale = 4.0 / math.sqrt(D)

    def one_block(packed):
        query_rows, id_rows, reader_rows = packed
        gathered = jnp.take(passages, id_rows, axis=0).astype(jnp.float32)
        scores = jnp.einsum('qd,qkd->qk', query_rows.astype(jnp.float32), gathered, precision=lax.Precision.HIGHEST) * score_scale
        log_retriever = log_normalize(scores)
        log_reader = log_normalize(reader_rows)
        reader_prob = jnp.exp(log_reader)
        retriever_prob = jnp.exp(log_retriever)
        divergence = lax.optimization_barrier(jnp.sum(reader_prob * (log_reader - log_retriever), axis=1))
        rounded = (retriever_prob - reader_prob).astype(jnp.bfloat16)
        rounded = lax.optimization_barrier(rounded)
        grads = jnp.einsum('qk,qkd->qd', rounded.astype(jnp.float32), gathered, precision=lax.Precision.HIGHEST) * score_scale
        return (divergence, grads)
    divergence, grads = lax.map(one_block, (questions.reshape(blocks, block_rows, D), candidate_ids.reshape(blocks, block_rows, K), reader_loglik.reshape(blocks, block_rows, K)))
    return (jnp.sum(divergence) / QUESTIONS, grads.reshape(QUESTIONS, D))
```

```python
import functools
import math

import jax
import jax.numpy as jnp
from jax import lax
from jax.experimental import pallas as pl
from jax.experimental.pallas import tpu as pltpu
from jax.sharding import PartitionSpec as P

MESH = pl.DeviceIdType.MESH
LANES = 128
VMEM_LIMIT = 56 * 1024 * 1024


class Place:
    def __init__(self, sizes):
        self.ny, self.nz, self.nx = sizes
        self.nb = self.nz * self.nx
        self.n = self.ny * 2 * self.nb
        index, bulk = lax.axis_index("index"), lax.axis_index("bulk")
        self.y, self.c = index // 2, index % 2
        self.z, self.x = bulk // self.nx, bulk % self.nx
        self.me = index * self.nb + bulk

    def number(self, y, c, z, x):
        return (y * 2 + c) * self.nb + z * self.nx + x

    def device(self, y, c, z, x):
        return (y * 2 + c, z * self.nx + x)

    def device_of(self, number):
        return (number // self.nb, number % self.nb)

    def plane(self):
        for a in range(self.ny):
            for b in range(self.nx):
                if a or b:
                    yield (a * self.nx + b, (self.y + a) % self.ny, (self.x + b) % self.nx)


def greet_all(place):
    barrier = pltpu.get_barrier_semaphore()

    def greet(i, carry):
        pl.semaphore_signal(
            barrier, inc=1, device_id=place.device_of((place.me + i) % place.n), device_id_type=MESH
        )
        return carry

    lax.fori_loop(1, place.n, greet, 0)
    pl.semaphore_wait(barrier, place.n - 1)


def to_all(place, src_of, dst, send_sem, recv_sem):
    def send(i, carry):
        other = (place.me + i) % place.n
        pltpu.make_async_remote_copy(
            src_ref=src_of(other), dst_ref=dst, send_sem=send_sem, recv_sem=recv_sem,
            device_id=place.device_of(other), device_id_type=MESH,
        ).start()
        return carry

    lax.fori_loop(1, place.n, send, 0)


def wait_bytes(ref, sem):
    pltpu.make_async_copy(ref, ref, sem).wait()


def gather_kernel(sizes, q_ref, id_ref, qall, idall, send_sem, recv_sem, id_send, id_recv):
    t = Place(sizes)
    rows, id_rows = q_ref.shape[0], id_ref.shape[0]
    greet_all(t)

    def block(number):
        return qall.at[pl.ds(pl.multiple_of(number * rows, rows), rows)]

    def copy(src, number, device):
        return pltpu.make_async_remote_copy(
            src_ref=src, dst_ref=block(number), send_sem=send_sem, recv_sem=recv_sem.at[number],
            device_id=device, device_id_type=MESH,
        )

    def arrived(number):
        wait_bytes(block(number), recv_sem.at[number])

    sibling = t.device(t.y, 1 - t.c, t.z, t.x)
    for i in range(1, t.nz):
        copy(q_ref, t.me, t.device(t.y, t.c, (t.z + i) % t.nz, t.x)).start()
    for _, y, x in t.plane():
        copy(q_ref, t.me, t.device(y, t.c, t.z, x)).start()
    copy(q_ref, t.me, sibling).start()
    my_ids = idall.at[pl.ds(pl.multiple_of(t.me * id_rows, id_rows), id_rows)]
    to_all(t, lambda other: id_ref, my_ids, id_send, id_recv)
    qall[pl.ds(pl.multiple_of(t.me * rows, rows), rows), :] = q_ref[...]
    idall[pl.ds(pl.multiple_of(t.me * id_rows, id_rows), id_rows), :] = id_ref[...]
    for i in range(1, t.nz):
        number = t.number(t.y, t.c, (t.z + i) % t.nz, t.x)
        arrived(number)
        for _, y, x in t.plane():
            copy(block(number), number, t.device(y, t.c, t.z, x)).start()
        copy(block(number), number, sibling).start()
    for i in range(t.nz):
        for _, y, x in t.plane():
            number = t.number(y, t.c, (t.z + i) % t.nz, x)
            arrived(number)
            copy(block(number), number, sibling).start()
    for i in range(t.nz):
        arrived(t.number(t.y, 1 - t.c, (t.z + i) % t.nz, t.x))
        for _, y, x in t.plane():
            arrived(t.number(y, 1 - t.c, (t.z + i) % t.nz, x))
    others = qall.at[pl.ds(0, (t.n - 1) * rows)]
    wait_bytes(others, send_sem)
    other_ids = idall.at[pl.ds(0, (t.n - 1) * id_rows)]
    wait_bytes(other_ids, id_recv)
    wait_bytes(other_ids, id_send)


def score_kernel(sizes, chunk, k, qall, p_ref, idall, out, s):
    t = Place(sizes)
    per, width = p_ref.shape
    tiles, group = per // LANES, LANES // k
    id_rows = idall.shape[0] // t.n
    rows = id_rows * group
    lane_group = lax.broadcasted_iota(jnp.int32, (id_rows, LANES), 1) // k

    def one_chunk(g, carry):
        q = qall[pl.ds(pl.multiple_of(g * chunk * rows, chunk * rows), chunk * rows), :]
        for h in range(0, tiles, 2):
            both = lax.dot_general(
                q, p_ref[h * LANES:(h + 2) * LANES, :],
                (((1,), (1,)), ((), ())), preferred_element_type=jnp.float32,
            )
            s[h] = both[:, :LANES]
            s[h + 1] = both[:, LANES:]

        def one_device(i, carry):
            at = pl.ds(pl.multiple_of((g * chunk + i) * id_rows, id_rows), id_rows)
            local = idall[at, :] - t.me * per
            own = (local >= 0) & (local < per)
            code = jnp.where(own, lane_group * tiles + local // LANES, -1)
            low = local & (LANES - 1)
            total = jnp.zeros((id_rows, LANES), jnp.float32)
            for j in range(group):
                for h in range(tiles):
                    piece = s[h, pl.ds(i * rows + j, id_rows, stride=group), :]
                    picked = jnp.take_along_axis(piece, low, axis=1)
                    total = jnp.where(code == j * tiles + h, picked, total)
            out[at, :] = total
            return carry

        return lax.fori_loop(0, chunk, one_device, carry)

    lax.fori_loop(0, t.n // chunk, one_chunk, 0)


def grouped(x, k, reduce, empty):
    group = lax.broadcasted_iota(jnp.int32, x.shape, 1) // k
    result = jnp.full(x.shape, empty, x.dtype)
    for j in range(x.shape[1] // k):
        value = reduce(jnp.where(group == j, x, empty), axis=1, keepdims=True)
        result = jnp.where(group == j, value, result)
    return result


def log_normalize(x, k):
    shifted = x - grouped(x, k, jnp.max, -jnp.inf)
    return shifted - jnp.log(grouped(jnp.exp(shifted), k, jnp.sum, 0.0))


def weight_kernel(sizes, k, scale, ps, reader, wall, mean, srecv, mine, mall,
                  s_send, s_recv, w_send, w_recv):
    t = Place(sizes)
    r = reader.shape[0]
    greet_all(t)

    def rows(number, count):
        return pl.ds(pl.multiple_of(number * count, count), count)

    to_all(t, lambda other: ps.at[rows(other, r)], srecv.at[rows(t.me, r)], s_send, s_recv)
    srecv[rows(t.me, r), :] = ps[rows(t.me, r), :]
    log_reader = log_normalize(reader[...], k)
    reader_prob = jnp.exp(log_reader)
    wait_bytes(srecv.at[pl.ds(0, (t.n - 1) * r)], s_recv)
    scores = jnp.sum(srecv[...].reshape(t.n, r, LANES), axis=0) * scale
    log_retriever = log_normalize(scores, k)
    weights = (jnp.exp(log_retriever) - reader_prob).astype(jnp.bfloat16).astype(jnp.float32)
    mine[0:r, :] = weights
    mine[r:2 * r, :] = reader_prob * (log_reader - log_retriever)
    to_all(t, lambda other: mine, mall.at[rows(t.me, 2 * r)], w_send, w_recv)
    mall[rows(t.me, 2 * r), :] = mine[...]
    wait_bytes(mall.at[pl.ds(0, (t.n - 1) * 2 * r)], w_recv)
    parts = mall[...].reshape(t.n, 2 * r, LANES)
    wall[...] = parts[:, :r, :].reshape(t.n * r, LANES)
    total = jnp.sum(jnp.sum(parts[:, r:, :], axis=0))
    mean[0, 0] = total / (t.n * r * LANES // k)
    wait_bytes(srecv.at[pl.ds(0, (t.n - 1) * r)], s_send)
    wait_bytes(mall.at[pl.ds(0, (t.n - 1) * 2 * r)], w_send)


def grad_kernel(sizes, chunk, k, wall, p_ref, idall, out, wd):
    t = Place(sizes)
    per, width = p_ref.shape
    tiles, group = per // LANES, LANES // k
    id_rows = idall.shape[0] // t.n
    rows = id_rows * group
    pair = 8 // group
    lane_group = lax.broadcasted_iota(jnp.int32, (id_rows, LANES), 1) // k
    row_part = lax.broadcasted_iota(jnp.int32, (id_rows, LANES), 0) % pair
    spot = lax.broadcasted_iota(jnp.int32, (8 * tiles, LANES), 0)
    place_in = lax.broadcasted_iota(jnp.int32, (LANES, LANES), 0)

    def one_chunk(g, carry):
        def one_device(i, carry):
            at = pl.ds(pl.multiple_of((g * chunk + i) * id_rows, id_rows), id_rows)
            local = idall[at, :] - t.me * per
            own = (local >= 0) & (local < per)
            code = jnp.where(own, (local // LANES) * 8 + row_part * group + lane_group, -1)
            low = local & (LANES - 1)
            w = wall[at, :]
            for a in range(0, id_rows, pair):
                left = jnp.concatenate(
                    [jnp.where(spot == code[b:b + 1, :], w[b:b + 1, :], 0.0) for b in range(a, a + pair)],
                    axis=1).astype(jnp.bfloat16)
                right = jnp.concatenate(
                    [jnp.where(place_in == low[b:b + 1, :], 1.0, 0.0) for b in range(a, a + pair)],
                    axis=1).astype(jnp.bfloat16)
                dense = lax.dot_general(
                    left, right, (((1,), (1,)), ((), ())), preferred_element_type=jnp.float32)
                to = pl.ds(pl.multiple_of(i * rows + a * group, 8), 8)
                for h in range(tiles):
                    wd[to, h * LANES:(h + 1) * LANES] = dense[h * 8:(h + 1) * 8, :]
            return carry

        lax.fori_loop(0, chunk, one_device, 0)
        out[pl.ds(pl.multiple_of(g * chunk * rows, chunk * rows), chunk * rows), :] = jnp.dot(
            wd[...].astype(jnp.bfloat16), p_ref[...], preferred_element_type=jnp.float32)
        return carry

    lax.fori_loop(0, t.n // chunk, one_chunk, 0)


def reduce_kernel(sizes, scale, g_ref, out, sib, acc, going, coming, zin,
                  sib_send, sib_recv, p_send, p_recv, z_send, z_recv):
    t = Place(sizes)
    rows = out.shape[0]
    greet_all(t)

    def span(number, count=1):
        return pl.ds(pl.multiple_of(number * rows, rows), count * rows)

    order = list(range(1, t.nz)) + [0]
    firsts = []
    for i in order:
        z = (t.z + i) % t.nz
        for y in range(t.ny):
            slot = i * t.ny + y
            copy = pltpu.make_async_remote_copy(
                src_ref=g_ref.at[span(t.number(y, 1 - t.c, z, 0), t.nx)],
                dst_ref=sib.at[span(y * t.nb + z * t.nx, t.nx)],
                send_sem=sib_send.at[slot], recv_sem=sib_recv.at[slot],
                device_id=t.device(t.y, 1 - t.c, t.z, t.x), device_id_type=MESH,
            )
            copy.start()
            firsts.append(copy)
    at = 0
    seconds = {}
    for i in order:
        z = (t.z + i) % t.nz
        for y in range(t.ny):
            firsts[at].wait_recv()
            at += 1

        def summed(y, x):
            return g_ref[span(t.number(y, t.c, z, x)), :] + sib[span(y * t.nb + z * t.nx + x), :]

        for o, y, x in t.plane():
            going[i, o] = summed(y, x).astype(jnp.bfloat16)
            copy = pltpu.make_async_remote_copy(
                src_ref=going.at[i, o], dst_ref=coming.at[i, o],
                send_sem=p_send.at[i, o], recv_sem=p_recv.at[i, o],
                device_id=t.device(y, t.c, t.z, x), device_id_type=MESH,
            )
            copy.start()
            seconds[i, o] = copy
        acc[i] = summed(t.y, t.x)
    thirds = []
    for i in order:
        total = acc[i]
        for o, _, _ in t.plane():
            seconds[i, o].wait_recv()
            total = total + coming[i, o].astype(jnp.float32)
        acc[i] = total
        if i:
            copy = pltpu.make_async_remote_copy(
                src_ref=acc.at[i], dst_ref=zin.at[i],
                send_sem=z_send.at[i], recv_sem=z_recv.at[i],
                device_id=t.device(t.y, t.c, (t.z + i) % t.nz, t.x), device_id_type=MESH,
            )
            copy.start()
            thirds.append((i, copy))
    total = acc[0]
    for i, copy in thirds:
        copy.wait_recv()
        total = total + zin[i]
    out[...] = total * scale
    for copy in firsts + list(seconds.values()) + [copy for _, copy in thirds]:
        copy.wait_send()


def solution(mesh):
    n_index, n_bulk = mesh.shape["index"], mesh.shape["bulk"]
    ny = n_index // 2
    nx = math.gcd(ny, n_bulk)
    sizes = (ny, n_bulk // nx, nx)
    nz = sizes[1]
    n = n_index * n_bulk
    vmem = pl.BlockSpec(memory_space=pltpu.VMEM)
    dma = pltpu.SemaphoreType.DMA

    def remote(number):
        return pltpu.CompilerParams(
            collective_id=number, has_side_effects=True, vmem_limit_bytes=VMEM_LIMIT)

    local = pltpu.CompilerParams(vmem_limit_bytes=VMEM_LIMIT)

    def body(questions, passages, candidate_ids, reader_loglik):
        rows, k = candidate_ids.shape
        width = passages.shape[1]
        per = passages.shape[0]
        id_rows = rows * k // LANES
        scale = 4.0 / math.sqrt(width)
        ids = candidate_ids.reshape(id_rows, LANES)
        reader = reader_loglik.reshape(id_rows, LANES)
        chunk = 8
        f32, bf16, i32 = jnp.float32, jnp.bfloat16, jnp.int32

        qall, idall = pl.pallas_call(
            functools.partial(gather_kernel, sizes),
            out_shape=(jax.ShapeDtypeStruct((n * rows, width), bf16),
                       jax.ShapeDtypeStruct((n * id_rows, LANES), i32)),
            in_specs=[vmem] * 2, out_specs=(vmem, vmem),
            scratch_shapes=[dma, dma((n,)), dma, dma],
            compiler_params=remote(0), name="gather_questions",
        )(questions, ids)
        partial = pl.pallas_call(
            functools.partial(score_kernel, sizes, chunk, k),
            out_shape=jax.ShapeDtypeStruct((n * id_rows, LANES), f32),
            in_specs=[vmem] * 3, out_specs=vmem,
            scratch_shapes=[pltpu.VMEM((per // LANES, chunk * rows, LANES), f32)],
            compiler_params=local, name="owner_scores",
        )(qall, passages, idall)
        wall, mean = pl.pallas_call(
            functools.partial(weight_kernel, sizes, k, scale),
            out_shape=(jax.ShapeDtypeStruct((n * id_rows, LANES), f32),
                       jax.ShapeDtypeStruct((1, 1), f32)),
            in_specs=[vmem] * 2, out_specs=(vmem, pl.BlockSpec(memory_space=pltpu.SMEM)),
            scratch_shapes=[pltpu.VMEM((n * id_rows, LANES), f32),
                            pltpu.VMEM((2 * id_rows, LANES), f32),
                            pltpu.VMEM((n * 2 * id_rows, LANES), f32),
                            dma, dma, dma, dma],
            compiler_params=remote(1), name="exchange_weights",
        )(partial, reader)
        grads = pl.pallas_call(
            functools.partial(grad_kernel, sizes, chunk, k),
            out_shape=jax.ShapeDtypeStruct((n * rows, width), f32),
            in_specs=[vmem] * 3, out_specs=vmem,
            scratch_shapes=[pltpu.VMEM((chunk * rows, per), f32)],
            compiler_params=local, name="owner_grads",
        )(wall, passages, idall)
        flat = ny * nx
        question_grads = pl.pallas_call(
            functools.partial(reduce_kernel, sizes, scale),
            out_shape=jax.ShapeDtypeStruct((rows, width), f32),
            in_specs=[vmem], out_specs=vmem,
            scratch_shapes=[pltpu.VMEM((n // 2 * rows, width), f32),
                            pltpu.VMEM((nz, rows, width), f32),
                            pltpu.VMEM((nz, flat, rows, width), bf16),
                            pltpu.VMEM((nz, flat, rows, width), bf16),
                            pltpu.VMEM((nz, rows, width), f32),
                            dma((nz * ny,)), dma((nz * ny,)),
                            dma((nz, flat)), dma((nz, flat)), dma((nz,)), dma((nz,))],
            compiler_params=remote(2), name="reduce_grads",
        )(grads)
        return mean[0, 0], question_grads

    placed = P(("index", "bulk"), None)
    return jax.shard_map(
        body, mesh=mesh, in_specs=(placed,) * 4, out_specs=(P(), placed), check_vma=False)
```

```python
import functools
import math

import jax
import jax.numpy as jnp
from jax import lax
from jax.experimental import pallas as pl
from jax.experimental.pallas import tpu as pltpu
from jax.sharding import PartitionSpec as P

MESH = pl.DeviceIdType.MESH
LANES = 128
SUB = 8
VMEM_LIMIT = 60 * 1024 * 1024


class Place:
    def __init__(self, sizes):
        self.ny, self.nz, self.nx = sizes
        self.flat = self.ny * self.nx
        self.chunk = 2 * self.flat
        self.n = self.chunk * self.nz
        index, bulk = lax.axis_index("index"), lax.axis_index("bulk")
        self.y, self.c = index // 2, index % 2
        self.z, self.x = bulk // self.nx, bulk % self.nx
        self.me = self.position(self.z, self.c, self.y, self.x)
        self.owner = index * self.nz * self.nx + bulk

    def position(self, z, c, y, x):
        return (z * 2 + c) * self.flat + y * self.nx + x

    def device(self, z, c, y, x):
        return (y * 2 + c, z * self.nx + x)

    def device_at(self, position):
        z, rest = position // self.chunk, position % self.chunk
        c, rest = rest // self.flat, rest % self.flat
        return self.device(z, c, rest // self.nx, rest % self.nx)

    def plane(self):
        for a in range(self.ny):
            for b in range(self.nx):
                if a or b:
                    yield (a * self.nx + b, (self.y + a) % self.ny, (self.x + b) % self.nx)


def wait_bytes(ref, sem):
    pltpu.make_async_copy(ref, ref, sem).wait()


def grouped(x, k, reduce, empty):
    group = lax.broadcasted_iota(jnp.int32, x.shape, 1) // k
    result = jnp.full(x.shape, empty, x.dtype)
    for j in range(x.shape[1] // k):
        value = reduce(jnp.where(group == j, x, empty), axis=1, keepdims=True)
        result = jnp.where(group == j, value, result)
    return result


def log_normalize(x, k):
    shifted = x - grouped(x, k, jnp.max, -jnp.inf)
    return shifted - jnp.log(grouped(jnp.exp(shifted), k, jnp.sum, 0.0))


def kernel(sizes, scale, hold, q_ref, p_hbm, id_ref, reader_ref, out, mean,
           p_ref, qall, idall, s, ps, srecv, mine, mall, onehot, wd, g, sib, acc, going, coming, zin, perm,
           p_sem, q_send, q_recv, id_send, id_recv, s_send, s_recv, w_send, w_recv,
           sib_send, sib_recv, p_send, p_recv, z_send, z_recv):
    t = Place(sizes)
    rows, k = id_ref.shape
    per, width = p_ref.shape
    tiles, group = per // LANES, LANES // k
    r8 = rows // group
    pair = 8 // group
    half = t.flat * rows
    f32, bf16 = jnp.float32, jnp.bfloat16

    def span(number, count):
        return pl.ds(pl.multiple_of(number * count, count), count)

    load = pltpu.make_async_copy(p_hbm, p_ref, p_sem)
    load.start()
    barrier = pltpu.get_barrier_semaphore()

    def greet(i, carry):
        pl.semaphore_signal(
            barrier, inc=1, device_id=t.device_at((t.me + i) % t.n), device_id_type=MESH)
        return carry

    lax.fori_loop(1, t.n, greet, 0)

    def packed(ref):
        return jnp.concatenate([ref[j * r8:(j + 1) * r8, :] for j in range(group)], axis=1)

    idall[span(t.me, r8), :] = packed(id_ref)
    qall[span(t.me, rows), :] = q_ref[...]
    log_reader = log_normalize(packed(reader_ref), k)
    reader_prob = jnp.exp(log_reader)
    pl.semaphore_wait(barrier, t.n - 1)

    def to_all(src, dst, send_sem, recv_sem):
        def send(i, carry):
            pltpu.make_async_remote_copy(
                src_ref=src, dst_ref=dst, send_sem=send_sem, recv_sem=recv_sem,
                device_id=t.device_at((t.me + i) % t.n), device_id_type=MESH,
            ).start()
            return carry

        lax.fori_loop(1, t.n, send, 0)

    def block(position):
        return qall.at[span(position, rows)]

    def give(src, position, device):
        pltpu.make_async_remote_copy(
            src_ref=src, dst_ref=block(position), send_sem=q_send, recv_sem=q_recv.at[position],
            device_id=device, device_id_type=MESH,
        ).start()

    def arrived(position):
        wait_bytes(block(position), q_recv.at[position])

    sibling = t.device(t.z, 1 - t.c, t.y, t.x)
    for i in range(1, t.nz):
        give(q_ref, t.me, t.device((t.z + i) % t.nz, t.c, t.y, t.x))
    for _, y, x in t.plane():
        give(q_ref, t.me, t.device(t.z, t.c, y, x))
    give(q_ref, t.me, sibling)
    to_all(idall.at[span(t.me, r8)], idall.at[span(t.me, r8)], id_send, id_recv)

    def pass_plane(i):
        for _, y, x in t.plane():
            position = t.position((t.z + i) % t.nz, t.c, y, x)
            arrived(position)
            give(block(position), position, sibling)

    pass_plane(0)
    for i in range(1, t.nz):
        position = t.position((t.z + i) % t.nz, t.c, t.y, t.x)
        arrived(position)
        for _, y, x in t.plane():
            give(block(position), position, t.device(t.z, t.c, y, x))
        give(block(position), position, sibling)
    wait_bytes(idall.at[pl.ds(0, (t.n - 1) * r8)], id_recv)
    load.wait()

    lane_group = lax.broadcasted_iota(jnp.int32, (r8, LANES), 1) // k
    row_part = lax.broadcasted_iota(jnp.int32, (r8, LANES), 0) % pair

    def parts_of(position):
        local = idall[span(position, r8), :] - t.owner * per
        own = (local >= 0) & (local < per)
        return own, local // LANES, local & (LANES - 1)

    def score(base):
        def one_sub(u, carry):
            first = base + u * SUB
            q = qall[pl.ds(pl.multiple_of(first * rows, SUB * rows), SUB * rows), :]
            for h in range(0, tiles, 2):
                both = lax.dot_general(
                    q, p_ref[h * LANES:(h + 2) * LANES, :],
                    (((1,), (1,)), ((), ())), preferred_element_type=f32)
                s[h] = both[:, :LANES]
                s[h + 1] = both[:, LANES:]

            def one_device(i, carry):
                position = first + i
                own, high, low = parts_of(position)
                code = jnp.where(own, lane_group * tiles + high, -1)
                total = jnp.zeros((r8, LANES), f32)
                for j in range(group):
                    for h in range(tiles):
                        piece = s[h, pl.ds(pl.multiple_of(i * rows + j * r8, r8), r8), :]
                        picked = jnp.take_along_axis(piece, low, axis=1)
                        total = jnp.where(code == j * tiles + h, picked, total)
                ps[span(position, r8), :] = total

                @pl.when(position != t.me)
                def _():
                    pltpu.make_async_remote_copy(
                        src_ref=ps.at[span(position, r8)], dst_ref=srecv.at[span(t.me, r8)],
                        send_sem=s_send, recv_sem=s_recv,
                        device_id=t.device_at(position), device_id_type=MESH,
                    ).start()

                @pl.when(position == t.me)
                def _():
                    srecv[span(t.me, r8), :] = total

                return carry

            return lax.fori_loop(0, SUB, one_device, carry)

        lax.fori_loop(0, t.chunk // SUB, one_sub, 0)

    for i in range(t.nz):
        if i + 1 < t.nz:
            pass_plane(i + 1)
        z = (t.z + i) % t.nz
        arrived(t.position(z, 1 - t.c, t.y, t.x))
        for _, y, x in t.plane():
            arrived(t.position(z, 1 - t.c, y, x))
        score(z * t.chunk)

    iota16 = lax.broadcasted_iota(jnp.int32, (16, LANES), 0)

    def spread(row):
        return jnp.broadcast_to(row, (16, LANES)).astype(bf16)

    one, zero = jnp.ones((16, LANES), bf16), jnp.zeros((16, LANES), bf16)

    def column(m):
        return (iota16 + 16 * m).astype(f32).astype(bf16)

    def build(base, slot):
        def one_device(i, carry):
            _, _, low = parts_of(base + i)
            low = low.astype(f32)
            for b in range(r8):
                row = spread(low[b:b + 1, :])
                at = pl.ds(pl.multiple_of(((slot + i) * (r8 // pair) + b // pair) * LANES, LANES), LANES)
                onehot[at, (b % pair) * LANES:(b % pair + 1) * LANES] = jnp.concatenate(
                    [jnp.where(column(m) == row, one, zero) for m in range(LANES // 16)],
                    axis=0)
            return carry

        lax.fori_loop(0, t.chunk, one_device, 0)

    order = list(range(1, t.nz)) + [0]

    def early(indices):
        if hold:
            for i in indices:
                z = (t.z + i) % t.nz
                build(z * t.chunk, z * t.chunk)

    early(order[:t.nz // 2])

    wait_bytes(srecv.at[pl.ds(0, (t.n - 1) * r8)], s_recv)
    scores = jnp.sum(srecv[...].reshape(t.n, r8, LANES), axis=0) * scale
    log_retriever = log_normalize(scores, k)
    weights = (jnp.exp(log_retriever) - reader_prob).astype(bf16).astype(f32)
    mine[0:r8, :] = weights
    mine[r8:2 * r8, :] = reader_prob * (log_reader - log_retriever)
    to_all(mine, mall.at[span(t.me, 2 * r8)], w_send, w_recv)
    mall[span(t.me, 2 * r8), :] = mine[...]
    early(order[t.nz // 2:])
    wait_bytes(mall.at[pl.ds(0, (t.n - 1) * 2 * r8)], w_recv)

    def grads(i):
        base = (t.z + i) % t.nz * t.chunk
        if not hold:
            build(base, 0)

        def one_sub(u, carry):
            def one_device(v, carry):
                position = base + u * SUB + v
                slot = position if hold else u * SUB + v
                own, high, _ = parts_of(position)
                code = jnp.where(own, high * 8 + row_part * group + lane_group, -1).astype(f32)
                w = mall[pl.ds(pl.multiple_of(position * 2 * r8, 2 * r8), r8), :]
                for a in range(0, r8 // pair, 2):
                    dense = []
                    for e in (a, a + 1):
                        left = []
                        for b in range(e * pair, (e + 1) * pair):
                            codes, values = spread(code[b:b + 1, :]), spread(w[b:b + 1, :])
                            left.append(jnp.concatenate(
                                [jnp.where(column(m) == codes, values, zero)
                                 for m in range(8 * tiles // 16)], axis=0))
                        right = onehot[pl.ds(pl.multiple_of((slot * (r8 // pair) + e) * LANES, LANES), LANES), :]
                        dense.append(lax.dot_general(
                            jnp.concatenate(left, axis=1), right,
                            (((1,), (1,)), ((), ())), preferred_element_type=f32))
                    to = pl.ds(pl.multiple_of(v * rows + a * 8, 16), 16)
                    for h in range(tiles):
                        wd[to, h * LANES:(h + 1) * LANES] = jnp.concatenate(
                            [d[h * 8:(h + 1) * 8, :] for d in dense], axis=0).astype(bf16)
                return carry

            lax.fori_loop(0, SUB, one_device, 0)
            g[i, pl.ds(pl.multiple_of(u * SUB * rows, SUB * rows), SUB * rows), :] = jnp.dot(
                wd[...], p_ref[...], preferred_element_type=f32)
            return carry

        lax.fori_loop(0, t.chunk // SUB, one_sub, 0)
        copy = pltpu.make_async_remote_copy(
            src_ref=g.at[i, span(1 - t.c, half)], dst_ref=sib.at[i],
            send_sem=sib_send.at[i], recv_sem=sib_recv.at[i],
            device_id=sibling, device_id_type=MESH)
        copy.start()
        return copy

    firsts, seconds, thirds = {}, {}, {}

    def summed(i, y, x):
        number = y * t.nx + x
        return (g[i, pl.ds(pl.multiple_of(t.c * half + number * rows, rows), rows), :]
                + sib[i, span(number, rows), :])

    def in_plane(i):
        firsts[i].wait_recv()
        for o, y, x in t.plane():
            going[i, o] = summed(i, y, x).astype(bf16)
            copy = pltpu.make_async_remote_copy(
                src_ref=going.at[i, o], dst_ref=coming.at[i, o],
                send_sem=p_send.at[i, o], recv_sem=p_recv.at[i, o],
                device_id=t.device(t.z, t.c, y, x), device_id_type=MESH)
            copy.start()
            seconds[i, o] = copy
        acc[i] = summed(i, t.y, t.x)

    def along_z(i):
        total = acc[i]
        for o, _, _ in t.plane():
            seconds[i, o].wait_recv()
            total = total + coming[i, o].astype(f32)
        acc[i] = total
        if i:
            copy = pltpu.make_async_remote_copy(
                src_ref=acc.at[i], dst_ref=zin.at[i],
                send_sem=z_send.at[i], recv_sem=z_recv.at[i],
                device_id=t.device((t.z + i) % t.nz, t.c, t.y, t.x), device_id_type=MESH)
            copy.start()
            thirds[i] = copy

    for step in range(t.nz + 2):
        if step < t.nz:
            firsts[order[step]] = grads(order[step])
        if 1 <= step <= t.nz:
            in_plane(order[step - 1])
        if 2 <= step:
            along_z(order[step - 2])
    total = acc[0]
    for i, copy in thirds.items():
        copy.wait_recv()
        total = total + zin[i]
    for l in range(width // LANES):
        perm[l] = total[:, l * LANES:(l + 1) * LANES]
    for l in range(width // LANES):
        for j in range(group):
            out[j * r8:(j + 1) * r8, l * LANES:(l + 1) * LANES] = perm[l, pl.ds(j, r8, stride=group), :]
    divergence = mall[...].reshape(t.n, 2 * r8, LANES)[:, r8:, :]
    mean[0, 0] = jnp.sum(jnp.sum(divergence, axis=0)) / (t.n * rows)

    wait_bytes(qall.at[pl.ds(0, (t.n - 1) * rows)], q_send)
    wait_bytes(idall.at[pl.ds(0, (t.n - 1) * r8)], id_send)
    wait_bytes(srecv.at[pl.ds(0, (t.n - 1) * r8)], s_send)
    wait_bytes(mall.at[pl.ds(0, (t.n - 1) * 2 * r8)], w_send)
    for copies in (firsts, seconds, thirds):
        for copy in copies.values():
            copy.wait_send()


def solution(mesh):
    n_index, n_bulk = mesh.shape["index"], mesh.shape["bulk"]
    ny = n_index // 2
    nx = math.gcd(ny, n_bulk)
    nz = n_bulk // nx
    flat = ny * nx
    n = n_index * n_bulk
    vmem = pl.BlockSpec(memory_space=pltpu.VMEM)
    dma = pltpu.SemaphoreType.DMA

    def body(questions, passages, candidate_ids, reader_loglik):
        rows, k = candidate_ids.shape
        per, width = passages.shape
        r8 = rows * k // LANES
        scale = 4.0 / math.sqrt(width)
        f32, bf16, i32 = jnp.float32, jnp.bfloat16, jnp.int32
        hold = n * rows * k * LANES * 2 <= 12 * 1024 * 1024
        held = n if hold else 2 * flat
        grads, mean = pl.pallas_call(
            functools.partial(kernel, (ny, nz, nx), scale, hold),
            out_shape=(jax.ShapeDtypeStruct((rows, width), f32), jax.ShapeDtypeStruct((1, 1), f32)),
            in_specs=[vmem, pl.BlockSpec(memory_space=pl.ANY), vmem, vmem],
            out_specs=(vmem, pl.BlockSpec(memory_space=pltpu.SMEM)),
            scratch_shapes=[
                pltpu.VMEM((per, width), bf16),
                pltpu.VMEM((n * rows, width), bf16),
                pltpu.VMEM((n * r8, LANES), i32),
                pltpu.VMEM((per // LANES, SUB * rows, LANES), f32),
                pltpu.VMEM((n * r8, LANES), f32),
                pltpu.VMEM((n * r8, LANES), f32),
                pltpu.VMEM((2 * r8, LANES), f32),
                pltpu.VMEM((n * 2 * r8, LANES), f32),
                pltpu.VMEM((held * rows * k // 2, 2 * LANES), bf16),
                pltpu.VMEM((SUB * rows, per), bf16),
                pltpu.VMEM((nz, 2 * flat * rows, width), f32),
                pltpu.VMEM((nz, flat * rows, width), f32),
                pltpu.VMEM((nz, rows, width), f32),
                pltpu.VMEM((nz, flat, rows, width), bf16),
                pltpu.VMEM((nz, flat, rows, width), bf16),
                pltpu.VMEM((nz, rows, width), f32),
                pltpu.VMEM((width // LANES, rows, LANES), f32),
                dma, dma, dma((n,)), dma, dma, dma, dma, dma, dma,
                dma((nz,)), dma((nz,)), dma((nz, flat)), dma((nz, flat)), dma((nz,)), dma((nz,)),
            ],
            compiler_params=pltpu.CompilerParams(
                collective_id=0, has_side_effects=True, vmem_limit_bytes=VMEM_LIMIT),
            name="retriever_step",
        )(questions, passages, candidate_ids, reader_loglik)
        return mean[0, 0], grads * scale

    placed = P(("index", "bulk"), None)
    return jax.shard_map(
        body, mesh=mesh, in_specs=(placed,) * 4, out_specs=(P(), placed), check_vma=False)
```

```python
import functools
import math

import jax
import jax.numpy as jnp
from jax import lax
from jax.experimental import pallas as pl
from jax.experimental.pallas import tpu as pltpu
from jax.sharding import PartitionSpec as P

MESH = pl.DeviceIdType.MESH
LANES = 128
SUB = 8
VMEM_LIMIT = 58 * 1024 * 1024


class Place:
    def __init__(self, sizes):
        self.ny, self.nz, self.nx = sizes
        self.flat = self.ny * self.nx
        self.chunk = 2 * self.flat
        self.n = self.chunk * self.nz
        index, bulk = lax.axis_index("index"), lax.axis_index("bulk")
        self.y, self.c = index // 2, index % 2
        self.z, self.x = bulk // self.nx, bulk % self.nx
        self.me = self.position(self.z, self.c, self.y, self.x)
        self.owner = index * self.nz * self.nx + bulk

    def position(self, z, c, y, x):
        return (z * 2 + c) * self.flat + y * self.nx + x

    def device(self, z, c, y, x):
        return (y * 2 + c, z * self.nx + x)

    def others(self, act):
        def one_plane(i, carry):
            z = lax.rem(self.z + i, self.nz)
            for c in (self.c, 1 - self.c):
                for a in range(self.ny):
                    for b in range(self.nx):
                        y, x = lax.rem(self.y + a, self.ny), lax.rem(self.x + b, self.nx)
                        if c is self.c and a == 0 and b == 0:
                            @pl.when(i > 0)
                            def _():
                                act(self.device(z, c, y, x))
                        else:
                            act(self.device(z, c, y, x))
            return carry

        lax.fori_loop(0, self.nz, one_plane, 0)

    def plane(self):
        for a in range(self.ny):
            for b in range(self.nx):
                if a or b:
                    yield (a * self.nx + b, (self.y + a) % self.ny, (self.x + b) % self.nx)


def wait_bytes(ref, sem):
    pltpu.make_async_copy(ref, ref, sem).wait()


def grouped(x, k, reduce, empty):
    group = lax.broadcasted_iota(jnp.int32, x.shape, 1) // k
    result = jnp.full(x.shape, empty, x.dtype)
    for j in range(x.shape[1] // k):
        value = reduce(jnp.where(group == j, x, empty), axis=1, keepdims=True)
        result = jnp.where(group == j, value, result)
    return result


def log_normalize(x, k):
    shifted = x - grouped(x, k, jnp.max, -jnp.inf)
    return shifted - jnp.log(grouped(jnp.exp(shifted), k, jnp.sum, 0.0))


def kernel(sizes, scale, hold, q_hbm, p_hbm, id_hbm, reader_hbm, out, mean,
           p_ref, id_ref, reader_ref, qall, idall, s, ps, srecv, mine, mall, onehot, wd, g, sib, acc, going, coming, zin, perm,
           p_sem, in_sem, q_send, q_recv, id_send, id_recv, s_send, s_recv, w_send, w_recv,
           sib_send, sib_recv, p_send, p_recv, z_send, z_recv):
    t = Place(sizes)
    rows, k = id_ref.shape
    per, width = p_ref.shape
    tiles, group = per // LANES, LANES // k
    r8 = rows // group
    pair = 8 // group
    half = t.flat * rows
    f32, bf16 = jnp.float32, jnp.bfloat16

    def span(number, count):
        return pl.ds(pl.multiple_of(number * count, count), count)

    mine_in = [
        pltpu.make_async_copy(id_hbm, id_ref, in_sem.at[0]),
        pltpu.make_async_copy(reader_hbm, reader_ref, in_sem.at[1]),
        pltpu.make_async_copy(q_hbm, qall.at[span(t.me, rows)], in_sem.at[2]),
    ]
    for copy in mine_in:
        copy.start()
    load = pltpu.make_async_copy(p_hbm, p_ref, p_sem)
    load.start()
    barrier = pltpu.get_barrier_semaphore()

    t.others(lambda device: pl.semaphore_signal(
        barrier, inc=1, device_id=device, device_id_type=MESH))

    def packed(ref):
        return jnp.concatenate([ref[j * r8:(j + 1) * r8, :] for j in range(group)], axis=1)

    for copy in mine_in:
        copy.wait()
    idall[span(t.me, r8), :] = packed(id_ref)
    log_reader = log_normalize(packed(reader_ref), k)
    reader_prob = jnp.exp(log_reader)
    pl.semaphore_wait(barrier, t.n - 1)

    def to_all(src, dst, send_sem, recv_sem):
        t.others(lambda device: pltpu.make_async_remote_copy(
            src_ref=src, dst_ref=dst, send_sem=send_sem, recv_sem=recv_sem,
            device_id=device, device_id_type=MESH).start())

    def block(position):
        return qall.at[span(position, rows)]

    def give(src, position, device):
        pltpu.make_async_remote_copy(
            src_ref=src, dst_ref=block(position), send_sem=q_send, recv_sem=q_recv.at[position],
            device_id=device, device_id_type=MESH,
        ).start()

    def arrived(position):
        wait_bytes(block(position), q_recv.at[position])

    sibling = t.device(t.z, 1 - t.c, t.y, t.x)
    for i in range(1, t.nz):
        give(block(t.me), t.me, t.device((t.z + i) % t.nz, t.c, t.y, t.x))
    for _, y, x in t.plane():
        give(block(t.me), t.me, t.device(t.z, t.c, y, x))
    give(block(t.me), t.me, sibling)
    to_all(idall.at[span(t.me, r8)], idall.at[span(t.me, r8)], id_send, id_recv)

    def pass_plane(i):
        for _, y, x in t.plane():
            position = t.position((t.z + i) % t.nz, t.c, y, x)
            arrived(position)
            give(block(position), position, sibling)

    pass_plane(0)
    for i in range(1, t.nz):
        position = t.position((t.z + i) % t.nz, t.c, t.y, t.x)
        arrived(position)
        for _, y, x in t.plane():
            give(block(position), position, t.device(t.z, t.c, y, x))
        give(block(position), position, sibling)
    wait_bytes(idall.at[pl.ds(0, (t.n - 1) * r8)], id_recv)
    load.wait()

    lane_group = lax.broadcasted_iota(jnp.int32, (r8, LANES), 1) // k
    row_part = lax.broadcasted_iota(jnp.int32, (r8, LANES), 0) % pair

    def parts_of(position):
        local = idall[span(position, r8), :] - t.owner * per
        own = (local >= 0) & (local < per)
        return own, local // LANES, local & (LANES - 1)

    def score(z):
        def one_sub(u, carry):
            first = z * t.chunk + u * SUB
            q = qall[pl.ds(pl.multiple_of(first * rows, SUB * rows), SUB * rows), :]
            codes, lows, totals = [], [], [None] * SUB
            for i in range(SUB):
                own, high, low = parts_of(first + i)
                codes.append(jnp.where(own, lane_group * tiles + high, -1))
                lows.append(low)
            for h in range(0, tiles, 2):
                s[h // 2] = lax.dot_general(
                    q, p_ref[h * LANES:(h + 2) * LANES, :],
                    (((1,), (1,)), ((), ())), preferred_element_type=f32)
            for h in range(tiles):
                for i in range(SUB):
                    for j in range(group):
                        piece = s[h // 2, i * rows + j * r8:i * rows + (j + 1) * r8,
                                  h % 2 * LANES:(h % 2 + 1) * LANES]
                        picked = jnp.take_along_axis(piece, lows[i], axis=1)
                        picked = jnp.where(codes[i] == j * tiles + h, picked, 0.0)
                        totals[i] = picked if totals[i] is None else totals[i] + picked
            for i in range(SUB):
                ps[span(first + i, r8), :] = totals[i]
            return carry

        lax.fori_loop(0, t.chunk // SUB, one_sub, 0)
        for c in range(2):
            for y in range(t.ny):
                for x in range(t.nx):
                    position = t.position(z, c, y, x)

                    @pl.when(position != t.me)
                    def _():
                        pltpu.make_async_remote_copy(
                            src_ref=ps.at[span(position, r8)], dst_ref=srecv.at[span(t.me, r8)],
                            send_sem=s_send, recv_sem=s_recv,
                            device_id=t.device(z, c, y, x), device_id_type=MESH,
                        ).start()

    def one_plane(i, carry):
        @pl.when(i + 1 < t.nz)
        def _():
            pass_plane(i + 1)

        z = lax.rem(t.z + i, t.nz)
        arrived(t.position(z, 1 - t.c, t.y, t.x))
        for _, y, x in t.plane():
            arrived(t.position(z, 1 - t.c, y, x))
        score(z)
        return carry

    lax.fori_loop(0, t.nz, one_plane, 0)
    srecv[span(t.me, r8), :] = ps[span(t.me, r8), :]

    iota16 = lax.broadcasted_iota(jnp.int32, (16, LANES), 0)

    def spread(row):
        return jnp.broadcast_to(row, (16, LANES)).astype(bf16)

    one, zero = jnp.ones((16, LANES), bf16), jnp.zeros((16, LANES), bf16)

    def column(m):
        return (iota16 + 16 * m).astype(f32).astype(bf16)

    def build(base, slot):
        def one_device(i, carry):
            _, _, low = parts_of(base + i)
            low = low.astype(f32)
            for b in range(r8):
                row = spread(low[b:b + 1, :])
                at = pl.ds(pl.multiple_of(((slot + i) * (r8 // pair) + b // pair) * LANES, LANES), LANES)
                onehot[at, (b % pair) * LANES:(b % pair + 1) * LANES] = jnp.concatenate(
                    [jnp.where(column(m) == row, one, zero) for m in range(LANES // 16)],
                    axis=0)
            return carry

        lax.fori_loop(0, t.chunk, one_device, 0)

    def early(first, last):
        def one(i, carry):
            base = lax.rem(t.z + 1 + i, t.nz) * t.chunk
            build(base, base)
            return carry

        if hold:
            lax.fori_loop(first, last, one, 0)

    early(0, t.nz // 2)

    wait_bytes(srecv.at[pl.ds(0, (t.n - 1) * r8)], s_recv)
    scores = jnp.sum(srecv[...].reshape(t.n, r8, LANES), axis=0) * scale
    log_retriever = log_normalize(scores, k)
    weights = (jnp.exp(log_retriever) - reader_prob).astype(bf16).astype(f32)
    mine[0:r8, :] = weights
    mine[r8:2 * r8, :] = reader_prob * (log_reader - log_retriever)
    to_all(mine, mall.at[span(t.me, 2 * r8)], w_send, w_recv)
    mall[span(t.me, 2 * r8), :] = mine[...]
    early(t.nz // 2, t.nz)
    wait_bytes(mall.at[pl.ds(0, (t.n - 1) * 2 * r8)], w_recv)

    def grads(i):
        base = (t.z + i) % t.nz * t.chunk
        if not hold:
            build(base, 0)

        def one_sub(u, carry):
            def one_device(v, carry):
                position = base + u * SUB + v
                slot = position if hold else u * SUB + v
                own, high, _ = parts_of(position)
                code = jnp.where(own, high * 8 + row_part * group + lane_group, -1).astype(f32)
                w = mall[pl.ds(pl.multiple_of(position * 2 * r8, 2 * r8), r8), :]
                for a in range(0, r8 // pair, 2):
                    dense = []
                    for e in (a, a + 1):
                        left = []
                        for b in range(e * pair, (e + 1) * pair):
                            codes, values = spread(code[b:b + 1, :]), spread(w[b:b + 1, :])
                            left.append(jnp.concatenate(
                                [jnp.where(column(m) == codes, values, zero)
                                 for m in range(8 * tiles // 16)], axis=0))
                        right = onehot[pl.ds(pl.multiple_of((slot * (r8 // pair) + e) * LANES, LANES), LANES), :]
                        dense.append(lax.dot_general(
                            jnp.concatenate(left, axis=1), right,
                            (((1,), (1,)), ((), ())), preferred_element_type=f32))
                    to = pl.ds(pl.multiple_of(v * rows + a * 8, 16), 16)
                    for h in range(tiles):
                        wd[to, h * LANES:(h + 1) * LANES] = jnp.concatenate(
                            [d[h * 8:(h + 1) * 8, :] for d in dense], axis=0).astype(bf16)
                return carry

            lax.fori_loop(0, SUB, one_device, 0)
            g[i, pl.ds(pl.multiple_of(u * SUB * rows, SUB * rows), SUB * rows), :] = jnp.dot(
                wd[...], p_ref[...], preferred_element_type=f32)
            return carry

        lax.fori_loop(0, t.chunk // SUB, one_sub, 0)
        first(i).start()

    def first(i):
        return pltpu.make_async_remote_copy(
            src_ref=g.at[i, span(1 - t.c, half)], dst_ref=sib.at[i],
            send_sem=sib_send.at[i], recv_sem=sib_recv.at[i],
            device_id=sibling, device_id_type=MESH)

    def second(i, o, y, x):
        return pltpu.make_async_remote_copy(
            src_ref=going.at[i, o], dst_ref=coming.at[i, o],
            send_sem=p_send.at[i, o], recv_sem=p_recv.at[i, o],
            device_id=t.device(t.z, t.c, y, x), device_id_type=MESH)

    def third(i):
        return pltpu.make_async_remote_copy(
            src_ref=acc.at[i], dst_ref=zin.at[i],
            send_sem=z_send.at[i], recv_sem=z_recv.at[i],
            device_id=t.device(lax.rem(t.z + i, t.nz), t.c, t.y, t.x), device_id_type=MESH)

    def summed(i, y, x):
        number = y * t.nx + x
        return (g[i, pl.ds(pl.multiple_of(t.c * half + number * rows, rows), rows), :]
                + sib[i, span(number, rows), :])

    def in_plane(i):
        first(i).wait_recv()
        for o, y, x in t.plane():
            going[i, o] = summed(i, y, x).astype(bf16)
            second(i, o, y, x).start()
        acc[i] = summed(i, t.y, t.x)

    def along_z(i):
        total = acc[i]
        for o, y, x in t.plane():
            second(i, o, y, x).wait_recv()
            total = total + coming[i, o].astype(f32)
        acc[i] = total

    def one_step(step, carry):
        grads(lax.rem(step + 1, t.nz))

        @pl.when(step >= 1)
        def _():
            in_plane(step)

        @pl.when(step >= 2)
        def _():
            along_z(step - 1)
            third(step - 1).start()

        return carry

    lax.fori_loop(0, t.nz, one_step, 0)
    in_plane(0)
    along_z(t.nz - 1)
    third(t.nz - 1).start()
    divergence = mall[...].reshape(t.n, 2 * r8, LANES)[:, r8:, :]
    mean[0, 0] = jnp.sum(jnp.sum(divergence, axis=0)) / (t.n * rows)
    along_z(0)
    total = acc[0]
    for i in range(1, t.nz):
        third(i).wait_recv()
        total = total + zin[i]
    for l in range(width // LANES):
        perm[l] = total[:, l * LANES:(l + 1) * LANES]
    for l in range(width // LANES):
        for j in range(group):
            out[j * r8:(j + 1) * r8, l * LANES:(l + 1) * LANES] = perm[l, pl.ds(j, r8, stride=group), :]
    wait_bytes(qall.at[pl.ds(0, (t.n - 1) * rows)], q_send)
    wait_bytes(idall.at[pl.ds(0, (t.n - 1) * r8)], id_send)
    wait_bytes(srecv.at[pl.ds(0, (t.n - 1) * r8)], s_send)
    wait_bytes(mall.at[pl.ds(0, (t.n - 1) * 2 * r8)], w_send)
    for i in range(t.nz):
        first(i).wait_send()
        for o, y, x in t.plane():
            second(i, o, y, x).wait_send()
        if i:
            third(i).wait_send()


def solution(mesh):
    n_index, n_bulk = mesh.shape["index"], mesh.shape["bulk"]
    ny = n_index // 2
    nx = math.gcd(ny, n_bulk)
    nz = n_bulk // nx
    flat = ny * nx
    n = n_index * n_bulk
    vmem = pl.BlockSpec(memory_space=pltpu.VMEM)
    dma = pltpu.SemaphoreType.DMA

    def body(questions, passages, candidate_ids, reader_loglik):
        rows, k = candidate_ids.shape
        per, width = passages.shape
        r8 = rows * k // LANES
        scale = 4.0 / math.sqrt(width)
        f32, bf16, i32 = jnp.float32, jnp.bfloat16, jnp.int32
        hold = n * rows * k * LANES * 2 <= 12 * 1024 * 1024
        held = n if hold else 2 * flat
        grads, mean = pl.pallas_call(
            functools.partial(kernel, (ny, nz, nx), scale, hold),
            out_shape=(jax.ShapeDtypeStruct((rows, width), f32), jax.ShapeDtypeStruct((1, 1), f32)),
            in_specs=[pl.BlockSpec(memory_space=pl.ANY)] * 4,
            out_specs=(vmem, pl.BlockSpec(memory_space=pltpu.SMEM)),
            scratch_shapes=[
                pltpu.VMEM((per, width), bf16),
                pltpu.VMEM((rows, k), i32),
                pltpu.VMEM((rows, k), f32),
                pltpu.VMEM((n * rows, width), bf16),
                pltpu.VMEM((n * r8, LANES), i32),
                pltpu.VMEM((per // LANES // 2, SUB * rows, 2 * LANES), f32),
                pltpu.VMEM((n * r8, LANES), f32),
                pltpu.VMEM((n * r8, LANES), f32),
                pltpu.VMEM((2 * r8, LANES), f32),
                pltpu.VMEM((n * 2 * r8, LANES), f32),
                pltpu.VMEM((held * rows * k // 2, 2 * LANES), bf16),
                pltpu.VMEM((SUB * rows, per), bf16),
                pltpu.VMEM((nz, 2 * flat * rows, width), f32),
                pltpu.VMEM((nz, flat * rows, width), f32),
                pltpu.VMEM((nz, rows, width), f32),
                pltpu.VMEM((nz, flat, rows, width), bf16),
                pltpu.VMEM((nz, flat, rows, width), bf16),
                pltpu.VMEM((nz, rows, width), f32),
                pltpu.VMEM((width // LANES, rows, LANES), f32),
                dma, dma((3,)), dma, dma((n,)), dma, dma, dma, dma, dma, dma,
                dma((nz,)), dma((nz,)), dma((nz, flat)), dma((nz, flat)), dma((nz,)), dma((nz,)),
            ],
            compiler_params=pltpu.CompilerParams(
                collective_id=0, has_side_effects=True, vmem_limit_bytes=VMEM_LIMIT),
            name="retriever_step",
        )(questions, passages, candidate_ids, reader_loglik)
        return mean[0, 0], grads * scale

    placed = P(("index", "bulk"), None)
    return jax.shard_map(
        body, mesh=mesh, in_specs=(placed,) * 4, out_specs=(P(), placed), check_vma=False)
```

```python
import functools
import math

import jax
import jax.numpy as jnp
from jax import lax
from jax.experimental import pallas as pl
from jax.experimental.pallas import tpu as pltpu
from jax.sharding import PartitionSpec as P

MESH = pl.DeviceIdType.MESH
LANES = 128
SUB = 8
VMEM_LIMIT = 58 * 1024 * 1024


class Place:
    def __init__(self, sizes):
        self.ny, self.nz, self.nx = sizes
        self.flat = self.ny * self.nx
        self.chunk = 2 * self.flat
        self.n = self.chunk * self.nz
        index, bulk = lax.axis_index("index"), lax.axis_index("bulk")
        self.y, self.c = index // 2, index % 2
        self.z, self.x = bulk // self.nx, bulk % self.nx
        self.me = self.position(self.z, self.c, self.y, self.x)
        self.owner = index * self.nz * self.nx + bulk

    def position(self, z, c, y, x):
        return (z * 2 + c) * self.flat + y * self.nx + x

    def device(self, z, c, y, x):
        return (y * 2 + c, z * self.nx + x)

    def others(self, act):
        def one_plane(i, carry):
            z = lax.rem(self.z + i, self.nz)
            for c in (self.c, 1 - self.c):
                for a in range(self.ny):
                    for b in range(self.nx):
                        y, x = lax.rem(self.y + a, self.ny), lax.rem(self.x + b, self.nx)
                        if c is self.c and a == 0 and b == 0:
                            @pl.when(i > 0)
                            def _():
                                act(self.device(z, c, y, x))
                        else:
                            act(self.device(z, c, y, x))
            return carry

        lax.fori_loop(0, self.nz, one_plane, 0)

    def plane(self):
        for a in range(self.ny):
            for b in range(self.nx):
                if a or b:
                    yield (a * self.nx + b, (self.y + a) % self.ny, (self.x + b) % self.nx)


def wait_bytes(ref, sem):
    pltpu.make_async_copy(ref, ref, sem).wait()


def grouped(x, k, reduce, empty):
    group = lax.broadcasted_iota(jnp.int32, x.shape, 1) // k
    result = jnp.full(x.shape, empty, x.dtype)
    for j in range(x.shape[1] // k):
        value = reduce(jnp.where(group == j, x, empty), axis=1, keepdims=True)
        result = jnp.where(group == j, value, result)
    return result


def log_normalize(x, k):
    shifted = x - grouped(x, k, jnp.max, -jnp.inf)
    return shifted - jnp.log(grouped(jnp.exp(shifted), k, jnp.sum, 0.0))


def kernel(sizes, scale, cap, q_hbm, p_hbm, id_hbm, reader_hbm, out, mean,
           p_ref, id_ref, reader_ref, qall, idall, rank, found, held, ps, srecv, mine, mall, g, sib, acc, going, coming, zin,
           p_sem, in_sem, q_send, q_recv, id_send, id_recv, s_send, s_recv, w_send, w_recv,
           sib_send, sib_recv, p_send, p_recv, z_send, z_recv):
    t = Place(sizes)
    rows, k = id_ref.shape
    per, width = p_ref.shape
    tiles, group = per // LANES, LANES // k
    r8 = rows // group
    half = t.flat * rows
    f32, bf16 = jnp.float32, jnp.bfloat16

    def span(number, count):
        return pl.ds(pl.multiple_of(number * count, count), count)

    mine_in = [
        pltpu.make_async_copy(id_hbm, id_ref, in_sem.at[0]),
        pltpu.make_async_copy(reader_hbm, reader_ref, in_sem.at[1]),
        pltpu.make_async_copy(q_hbm, qall.at[span(t.me, rows)], in_sem.at[2]),
    ]
    for copy in mine_in:
        copy.start()
    load = pltpu.make_async_copy(p_hbm, p_ref, p_sem)
    load.start()
    barrier = pltpu.get_barrier_semaphore()

    t.others(lambda device: pl.semaphore_signal(
        barrier, inc=1, device_id=device, device_id_type=MESH))

    def packed(ref):
        return jnp.concatenate([ref[j * r8:(j + 1) * r8, :] for j in range(group)], axis=1)

    for copy in mine_in:
        copy.wait()
    idall[span(t.me, r8), :] = packed(id_ref)
    log_reader = log_normalize(packed(reader_ref), k)
    reader_prob = jnp.exp(log_reader)
    pl.semaphore_wait(barrier, t.n - 1)

    def to_all(src, dst, send_sem, recv_sem):
        t.others(lambda device: pltpu.make_async_remote_copy(
            src_ref=src, dst_ref=dst, send_sem=send_sem, recv_sem=recv_sem,
            device_id=device, device_id_type=MESH).start())

    def block(position):
        return qall.at[span(position, rows)]

    def give(src, position, device):
        pltpu.make_async_remote_copy(
            src_ref=src, dst_ref=block(position), send_sem=q_send, recv_sem=q_recv.at[position],
            device_id=device, device_id_type=MESH,
        ).start()

    def arrived(position):
        wait_bytes(block(position), q_recv.at[position])

    sibling = t.device(t.z, 1 - t.c, t.y, t.x)
    for i in range(1, t.nz):
        give(block(t.me), t.me, t.device((t.z + i) % t.nz, t.c, t.y, t.x))
    for _, y, x in t.plane():
        give(block(t.me), t.me, t.device(t.z, t.c, y, x))
    give(block(t.me), t.me, sibling)
    to_all(idall.at[span(t.me, r8)], idall.at[span(t.me, r8)], id_send, id_recv)

    for i in range(1, t.nz):
        position = t.position((t.z + i) % t.nz, t.c, t.y, t.x)
        arrived(position)
        for _, y, x in t.plane():
            give(block(position), position, t.device(t.z, t.c, y, x))
        give(block(position), position, sibling)

    def pass_plane(z):
        for _, y, x in t.plane():
            position = t.position(z, t.c, y, x)
            arrived(position)
            give(block(position), position, sibling)

    wait_bytes(idall.at[pl.ds(0, (t.n - 1) * r8)], id_recv)

    def iota(shape, dim):
        return lax.broadcasted_iota(jnp.int32, shape, dim)

    lane_group = iota((r8, LANES), 1) // k
    slots = iota((cap, LANES), 0).astype(f32)
    lanes = iota((cap, LANES), 1).astype(f32)
    count = SUB * r8
    before = (iota((LANES, LANES), 0) < iota((LANES, LANES), 1)).astype(f32).astype(bf16)
    row, col = iota((count, count), 0), iota((count, count), 1)
    above = ((row // r8 == col // r8) & (col < row)).astype(f32).astype(bf16)

    def one_rank(u, carry):
        at = pl.ds(pl.multiple_of(u * count, count), count)
        local = idall[at, :] - t.owner * per
        own = (local >= 0) & (local < per)
        ones = own.astype(f32).astype(bf16)
        earlier = jnp.dot(ones, before, preferred_element_type=f32)
        rows_above = jnp.sum(jnp.dot(above, ones, preferred_element_type=f32), axis=1, keepdims=True)
        rank[at, :] = jnp.where(own, earlier + rows_above, -1.0)
        return carry

    lax.fori_loop(0, t.n // SUB, one_rank, 0)
    load.wait()
    held[t.n * cap:, :] = jnp.zeros((LANES, width), bf16)

    def fetch(z):
        def one_sub(u, carry):
            first = z * t.chunk + u * SUB
            for v in range(SUB):
                at = span(first + v, r8)
                spot = rank[at, :]
                value = (idall[at, :] - t.owner * per + 1).astype(f32)
                chosen = jnp.zeros((cap, LANES), f32)
                for b in range(r8):
                    chosen = jnp.where(slots == spot[b:b + 1, :], value[b:b + 1, :], chosen)
                wanted = jnp.sum(chosen, axis=1, keepdims=True) - 1.0
                for h in range(tiles):
                    found[v * cap:(v + 1) * cap, h * LANES:(h + 1) * LANES] = jnp.where(
                        lanes == wanted - float(h * LANES), 1.0, 0.0).astype(bf16)
            held[pl.ds(pl.multiple_of(first * cap, SUB * cap), SUB * cap), :] = jnp.dot(
                found[...], p_ref[...], preferred_element_type=f32).astype(bf16)
            return carry

        lax.fori_loop(0, t.chunk // SUB, one_sub, 0)

    def score(z):
        def one_sub(u, carry):
            first = z * t.chunk + u * SUB
            for v in range(SUB):
                position = first + v
                products = lax.dot_general(
                    qall[span(position, rows), :], held[pl.ds(pl.multiple_of(position * cap, cap), LANES), :],
                    (((1,), (1,)), ((), ())), preferred_element_type=f32)
                spot = rank[span(position, r8), :].astype(jnp.int32)
                at = jnp.maximum(spot, 0)
                total = jnp.zeros((r8, LANES), f32)
                for j in range(group):
                    picked = jnp.take_along_axis(products[j * r8:(j + 1) * r8, :], at, axis=1)
                    total = jnp.where((spot >= 0) & (lane_group == j), picked, total)
                ps[span(position, r8), :] = total
            return carry

        lax.fori_loop(0, t.chunk // SUB, one_sub, 0)
        for c in range(2):
            for y in range(t.ny):
                for x in range(t.nx):
                    position = t.position(z, c, y, x)

                    @pl.when(position != t.me)
                    def _():
                        pltpu.make_async_remote_copy(
                            src_ref=ps.at[span(position, r8)], dst_ref=srecv.at[span(t.me, r8)],
                            send_sem=s_send, recv_sem=s_recv,
                            device_id=t.device(z, c, y, x), device_id_type=MESH,
                        ).start()

    def weigh():
        srecv[span(t.me, r8), :] = ps[span(t.me, r8), :]
        wait_bytes(srecv.at[pl.ds(0, (t.n - 1) * r8)], s_recv)
        scores = jnp.sum(srecv[...].reshape(t.n, r8, LANES), axis=0) * scale
        log_retriever = log_normalize(scores, k)
        weights = (jnp.exp(log_retriever) - reader_prob).astype(bf16).astype(f32)
        mine[0:r8, :] = weights
        mine[r8:2 * r8, :] = reader_prob * (log_reader - log_retriever)
        to_all(mine, mall.at[span(t.me, 2 * r8)], w_send, w_recv.at[t.z])
        mall[span(t.me, 2 * r8), :] = mine[...]

    def one_plane(step, carry):
        @pl.when(step < t.nz)
        def _():
            pass_plane(step)
            fetch(step)

            arrived(t.position(step, 1 - t.c, t.y, t.x))
            for _, y, x in t.plane():
                arrived(t.position(step, 1 - t.c, y, x))
            score(step)

        @pl.when(step == t.z + 2)
        def _():
            weigh()

        return carry

    lax.fori_loop(0, t.nz + 2, one_plane, 0)

    at_row = iota((rows, r8 * LANES), 1)
    pick = (iota((rows, r8 * LANES), 0) == at_row % LANES // k * r8 + at_row // LANES).astype(f32).astype(bf16)

    def grads(i):
        z = lax.rem(t.z + i, t.nz)
        weights_of = lambda count: wait_bytes(
            mall.at[pl.ds(pl.multiple_of(z * t.chunk * 2 * r8, 2 * r8), count * 2 * r8)], w_recv.at[z])

        @pl.when(i != 0)
        def _():
            weights_of(t.chunk)

        @pl.when(i == 0)
        def _():
            weights_of(t.chunk - 1)

        def one_sub(u, carry):
            for v in range(SUB):
                position = z * t.chunk + u * SUB + v
                spot = rank[span(position, r8), :]
                w = mall[pl.ds(pl.multiple_of(position * 2 * r8, 2 * r8), r8), :]
                spread = jnp.concatenate(
                    [jnp.where(slots == spot[b:b + 1, :], w[b:b + 1, :], 0.0).astype(bf16) for b in range(r8)],
                    axis=1)
                by_slot = lax.dot_general(
                    pick, spread, (((1,), (1,)), ((), ())), preferred_element_type=f32).astype(bf16)
                g[i, pl.ds(pl.multiple_of((u * SUB + v) * rows, rows), rows), :] = jnp.dot(
                    by_slot, held[pl.ds(pl.multiple_of(position * cap, cap), cap), :],
                    preferred_element_type=f32)
            return carry

        lax.fori_loop(0, t.chunk // SUB, one_sub, 0)
        first(i).start()

    def first(i):
        return pltpu.make_async_remote_copy(
            src_ref=g.at[i, span(1 - t.c, half)], dst_ref=sib.at[i],
            send_sem=sib_send.at[i], recv_sem=sib_recv.at[i],
            device_id=sibling, device_id_type=MESH)

    def second(i, o, y, x):
        return pltpu.make_async_remote_copy(
            src_ref=going.at[i, o], dst_ref=coming.at[i, o],
            send_sem=p_send.at[i, o], recv_sem=p_recv.at[i, o],
            device_id=t.device(t.z, t.c, y, x), device_id_type=MESH)

    def third(i):
        return pltpu.make_async_remote_copy(
            src_ref=acc.at[i], dst_ref=zin.at[i],
            send_sem=z_send.at[i], recv_sem=z_recv.at[i],
            device_id=t.device(lax.rem(t.z + i, t.nz), t.c, t.y, t.x), device_id_type=MESH)

    def summed(i, y, x):
        number = y * t.nx + x
        return (g[i, pl.ds(pl.multiple_of(t.c * half + number * rows, rows), rows), :]
                + sib[i, span(number, rows), :])

    def in_plane(i):
        first(i).wait_recv()
        for o, y, x in t.plane():
            going[i, o] = summed(i, y, x).astype(bf16)
            second(i, o, y, x).start()
        acc[i] = summed(i, t.y, t.x)

    def along_z(i):
        total = acc[i]
        for o, y, x in t.plane():
            second(i, o, y, x).wait_recv()
            total = total + coming[i, o].astype(f32)
        acc[i] = total

    def turn(step):
        z = step + (step >= t.z).astype(jnp.int32)
        return jnp.where(step >= t.nz - 1, 0, lax.rem(z - t.z + t.nz, t.nz))

    def one_step(step, carry):
        grads(turn(step))

        @pl.when(step >= 1)
        def _():
            in_plane(turn(step - 1))

        @pl.when(step >= 2)
        def _():
            along_z(turn(step - 2))
            third(turn(step - 2)).start()

        return carry

    lax.fori_loop(0, t.nz, one_step, 0)
    in_plane(0)
    last = turn(jnp.int32(t.nz - 2))
    along_z(last)
    third(last).start()
    divergence = mall[...].reshape(t.n, 2 * r8, LANES)[:, r8:, :]
    mean[0, 0] = jnp.sum(jnp.sum(divergence, axis=0)) / (t.n * rows)
    along_z(0)
    total = acc[0]
    for i in range(1, t.nz):
        third(i).wait_recv()
        total = total + zin[i]
    out[...] = total

    wait_bytes(qall.at[pl.ds(0, (t.n - 1) * rows)], q_send)
    wait_bytes(idall.at[pl.ds(0, (t.n - 1) * r8)], id_send)
    wait_bytes(srecv.at[pl.ds(0, (t.n - 1) * r8)], s_send)
    wait_bytes(mall.at[pl.ds(0, (t.n - 1) * 2 * r8)], w_send)
    for i in range(t.nz):
        first(i).wait_send()
        for o, y, x in t.plane():
            second(i, o, y, x).wait_send()
        if i:
            third(i).wait_send()


def solution(mesh):
    n_index, n_bulk = mesh.shape["index"], mesh.shape["bulk"]
    ny = n_index // 2
    nx = math.gcd(ny, n_bulk)
    nz = n_bulk // nx
    flat = ny * nx
    n = n_index * n_bulk
    vmem = pl.BlockSpec(memory_space=pltpu.VMEM)
    dma = pltpu.SemaphoreType.DMA

    def body(questions, passages, candidate_ids, reader_loglik):
        rows, k = candidate_ids.shape
        per, width = passages.shape
        r8 = rows * k // LANES
        scale = 4.0 / math.sqrt(width)
        f32, bf16, i32 = jnp.float32, jnp.bfloat16, jnp.int32
        cap = 2 * rows * k // n
        grads, mean = pl.pallas_call(
            functools.partial(kernel, (ny, nz, nx), scale, cap),
            out_shape=(jax.ShapeDtypeStruct((rows, width), f32), jax.ShapeDtypeStruct((1, 1), f32)),
            in_specs=[pl.BlockSpec(memory_space=pl.ANY)] * 4,
            out_specs=(vmem, pl.BlockSpec(memory_space=pltpu.SMEM)),
            scratch_shapes=[
                pltpu.VMEM((per, width), bf16),
                pltpu.VMEM((rows, k), i32),
                pltpu.VMEM((rows, k), f32),
                pltpu.VMEM((n * rows, width), bf16),
                pltpu.VMEM((n * r8, LANES), i32),
                pltpu.VMEM((n * r8, LANES), f32),
                pltpu.VMEM((SUB * cap, per), bf16),
                pltpu.VMEM((n * cap + LANES, width), bf16),
                pltpu.VMEM((n * r8, LANES), f32),
                pltpu.VMEM((n * r8, LANES), f32),
                pltpu.VMEM((2 * r8, LANES), f32),
                pltpu.VMEM((n * 2 * r8, LANES), f32),
                pltpu.VMEM((nz, 2 * flat * rows, width), f32),
                pltpu.VMEM((nz, flat * rows, width), f32),
                pltpu.VMEM((nz, rows, width), f32),
                pltpu.VMEM((nz, flat, rows, width), bf16),
                pltpu.VMEM((nz, flat, rows, width), bf16),
                pltpu.VMEM((nz, rows, width), f32),
                dma, dma((3,)), dma, dma((n,)), dma, dma, dma, dma, dma, dma((nz,)),
                dma((nz,)), dma((nz,)), dma((nz, flat)), dma((nz, flat)), dma((nz,)), dma((nz,)),
            ],
            compiler_params=pltpu.CompilerParams(
                collective_id=0, has_side_effects=True, vmem_limit_bytes=VMEM_LIMIT),
            name="retriever_step",
        )(questions, passages, candidate_ids, reader_loglik)
        return mean[0, 0], grads * scale

    placed = P(("index", "bulk"), None)
    return jax.shard_map(
        body, mesh=mesh, in_specs=(placed,) * 4, out_specs=(P(), placed), check_vma=False)
```

```python
import functools
import math

import jax
import jax.numpy as jnp
from jax import lax
from jax.experimental import pallas as pl
from jax.experimental.pallas import tpu as pltpu
from jax.sharding import PartitionSpec as P

MESH = pl.DeviceIdType.MESH
LANES = 128
SUB = 8
VMEM_LIMIT = 58 * 1024 * 1024


class Place:
    def __init__(self, sizes):
        self.ny, self.nz, self.nx = sizes
        self.flat = self.ny * self.nx
        self.chunk = 2 * self.flat
        self.n = self.chunk * self.nz
        index, bulk = lax.axis_index("index"), lax.axis_index("bulk")
        self.y, self.c = index // 2, index % 2
        self.z, self.x = bulk // self.nx, bulk % self.nx
        self.me = self.position(self.z, self.c, self.y, self.x)
        self.mine = self.small(self.z, self.c, self.y, self.x)
        self.owner = index * self.nz * self.nx + bulk

    def position(self, z, c, y, x):
        return (z * 2 + c) * self.flat + y * self.nx + x

    def device(self, z, c, y, x):
        return (y * 2 + c, z * self.nx + x)

    def small(self, z, c, y, x):
        return ((c * self.ny + y) * self.nx + x) * self.nz + z

    def plane(self):
        for a in range(self.ny):
            for b in range(self.nx):
                if a or b:
                    yield (a * self.nx + b, (self.y + a) % self.ny, (self.x + b) % self.nx)


def wait_bytes(ref, sem):
    pltpu.make_async_copy(ref, ref, sem).wait()


def grouped(x, k, reduce, empty):
    group = lax.broadcasted_iota(jnp.int32, x.shape, 1) // k
    result = jnp.full(x.shape, empty, x.dtype)
    for j in range(x.shape[1] // k):
        value = reduce(jnp.where(group == j, x, empty), axis=1, keepdims=True)
        result = jnp.where(group == j, value, result)
    return result


def log_normalize(x, k):
    shifted = x - grouped(x, k, jnp.max, -jnp.inf)
    return shifted - jnp.log(grouped(jnp.exp(shifted), k, jnp.sum, 0.0))


def kernel(sizes, scale, cap, q_hbm, p_hbm, id_hbm, reader_hbm, out, mean,
           p_ref, id_ref, reader_ref, qall, idall, rank, found, held, ps, s1, s2, s2out, s3, mall, g, sib, acc, going, coming, zin,
           p_sem, in_sem, q_send, q_recv, q_sib, id_send, id_z, id_plane, id_sib,
           s_send, s_recv, w_send, w_z, w_plane, w_sib,
           sib_send, sib_recv, p_send, p_recv, z_send, z_recv):
    t = Place(sizes)
    rows, k = id_ref.shape
    per, width = p_ref.shape
    tiles, group = per // LANES, LANES // k
    r8 = rows // group
    half = t.flat * rows
    f32, bf16 = jnp.float32, jnp.bfloat16
    id_sems, w_sems = (id_send, id_z, id_plane, id_sib), (w_send, w_z, w_plane, w_sib)

    def span(number, count):
        return pl.ds(pl.multiple_of(number * count, count), count)

    mine_in = [
        pltpu.make_async_copy(id_hbm, id_ref, in_sem.at[0]),
        pltpu.make_async_copy(reader_hbm, reader_ref, in_sem.at[1]),
        pltpu.make_async_copy(q_hbm, qall.at[span(t.me, rows)], in_sem.at[2]),
    ]
    for copy in mine_in:
        copy.start()
    load = pltpu.make_async_copy(p_hbm, p_ref, p_sem)
    load.start()
    barrier = pltpu.get_barrier_semaphore()

    sibling = t.device(t.z, 1 - t.c, t.y, t.x)
    column = [(i, t.device((t.z + i) % t.nz, t.c, t.y, t.x)) for i in range(1, t.nz)]
    around = [(o, t.device(t.z, t.c, y, x)) for o, y, x in t.plane()]
    near = [sibling] + [device for _, device in column + around]
    for device in near:
        pl.semaphore_signal(barrier, inc=1, device_id=device, device_id_type=MESH)

    def packed(ref):
        return jnp.concatenate([ref[j * r8:(j + 1) * r8, :] for j in range(group)], axis=1)

    for copy in mine_in:
        copy.wait()
    idall[span(t.mine, r8), :] = packed(id_ref)
    log_reader = log_normalize(packed(reader_ref), k)
    reader_prob = jnp.exp(log_reader)
    pl.semaphore_wait(barrier, len(near))

    def send(src, dst, send_sem, recv_sem, device):
        copy = pltpu.make_async_remote_copy(
            src_ref=src, dst_ref=dst, send_sem=send_sem, recv_sem=recv_sem,
            device_id=device, device_id_type=MESH)
        copy.start()

    def share_z(ref, count, sems):
        at = ref.at[span(t.mine, count)]
        for i, device in column:
            send(at, at, sems[0], sems[1].at[i], device)

    def share_plane(ref, count, sems):
        for i in range(1, t.nz):
            z = (t.z - i + t.nz) % t.nz
            wait_bytes(ref.at[span(t.small(z, t.c, t.y, t.x), count)], sems[1].at[i])
        at = ref.at[span(t.mine // t.nz, t.nz * count)]
        for o, device in around:
            send(at, at, sems[0], sems[2].at[o], device)

    def share_sibling(ref, count, sems):
        for o, y, x in t.plane():
            y, x = (2 * t.y - y + t.ny) % t.ny, (2 * t.x - x + t.nx) % t.nx
            wait_bytes(ref.at[span(t.small(0, t.c, y, x) // t.nz, t.nz * count)], sems[2].at[o])
        at = ref.at[span(t.c, t.flat * t.nz * count)]
        send(at, at, sems[0], sems[3], sibling)

    def share_done(ref, count, sems):
        wait_bytes(ref.at[span(1 - t.c, t.flat * t.nz * count)], sems[3])

    def block(position):
        return qall.at[span(position, rows)]

    def give(src, position, device):
        pltpu.make_async_remote_copy(
            src_ref=src, dst_ref=block(position), send_sem=q_send, recv_sem=q_recv.at[position],
            device_id=device, device_id_type=MESH,
        ).start()

    def arrived(position):
        wait_bytes(block(position), q_recv.at[position])

    share_z(idall, r8, id_sems)
    for _, device in column + around:
        give(block(t.me), t.me, device)
    share_plane(idall, r8, id_sems)
    for i in range(1, t.nz):
        position = t.position((t.z + i) % t.nz, t.c, t.y, t.x)
        arrived(position)
        for _, device in around:
            give(block(position), position, device)
    share_sibling(idall, r8, id_sems)

    def side(z, c):
        return qall.at[span(z * 2 + c, half)]

    def pass_plane(z):
        for _, y, x in t.plane():
            arrived(t.position(z, t.c, y, x))
        send(side(z, t.c), side(z, t.c), q_send, q_sib.at[z], sibling)

    pass_plane(t.z)
    share_done(idall, r8, id_sems)

    def iota(shape, dim):
        return lax.broadcasted_iota(jnp.int32, shape, dim)

    lane_group = iota((r8, LANES), 1) // k
    slots = iota((cap, LANES), 0).astype(f32)
    lanes = iota((cap, LANES), 1).astype(f32)
    count = SUB * r8
    before = (iota((LANES, LANES), 0) < iota((LANES, LANES), 1)).astype(f32).astype(bf16)
    row, col = iota((count, count), 0), iota((count, count), 1)
    above = ((row // r8 == col // r8) & (col < row)).astype(f32).astype(bf16)

    def one_rank(u, carry):
        at = pl.ds(pl.multiple_of(u * count, count), count)
        local = idall[at, :] - t.owner * per
        own = (local >= 0) & (local < per)
        ones = own.astype(f32).astype(bf16)
        earlier = jnp.dot(ones, before, preferred_element_type=f32)
        rows_above = jnp.sum(jnp.dot(above, ones, preferred_element_type=f32), axis=1, keepdims=True)
        rank[at, :] = jnp.where(own, earlier + rows_above, -1.0)
        return carry

    lax.fori_loop(0, t.n // SUB, one_rank, 0)
    load.wait()
    held[t.n * cap:, :] = jnp.zeros((LANES, width), bf16)

    def fetch(z):
        def one_sub(u, carry):
            first = z * t.chunk + u * SUB
            for v in range(SUB):
                at = span((u * SUB + v) * t.nz + z, r8)
                spot = rank[at, :]
                value = (idall[at, :] - t.owner * per + 1).astype(f32)
                chosen = jnp.zeros((cap, LANES), f32)
                for b in range(r8):
                    chosen = jnp.where(slots == spot[b:b + 1, :], value[b:b + 1, :], chosen)
                wanted = jnp.sum(chosen, axis=1, keepdims=True) - 1.0
                wanted = jnp.broadcast_to(wanted, (cap, LANES))
                high = jnp.floor(wanted * (1.0 / LANES))
                low_hot = jnp.where(lanes == wanted - high * LANES, 1.0, 0.0).astype(bf16)
                high = high.astype(bf16)
                for h in range(tiles):
                    found[v * cap:(v + 1) * cap, h * LANES:(h + 1) * LANES] = jnp.where(
                        high == jnp.full((cap, LANES), h, bf16), low_hot, jnp.zeros_like(low_hot))
            held[pl.ds(pl.multiple_of(first * cap, SUB * cap), SUB * cap), :] = jnp.dot(
                found[...], p_ref[...], preferred_element_type=f32).astype(bf16)
            return carry

        lax.fori_loop(0, t.chunk // SUB, one_sub, 0)

    def score(z):
        def one_sub(u, carry):
            first = z * t.chunk + u * SUB
            for v in range(SUB):
                position = first + v
                products = lax.dot_general(
                    qall[span(position, rows), :], held[pl.ds(pl.multiple_of(position * cap, cap), LANES), :],
                    (((1,), (1,)), ((), ())), preferred_element_type=f32)
                small = (u * SUB + v) * t.nz + z
                spot = rank[span(small, r8), :].astype(jnp.int32)
                at = jnp.maximum(spot, 0)
                total = jnp.zeros((r8, LANES), f32)
                for j in range(group):
                    picked = jnp.take_along_axis(products[j * r8:(j + 1) * r8, :], at, axis=1)
                    total = jnp.where((spot >= 0) & (lane_group == j), picked, total)
                ps[span(small, r8), :] = total
            return carry

        lax.fori_loop(0, t.chunk // SUB, one_sub, 0)
    def one_fetch(i, carry):
        z = lax.rem(t.z + i, t.nz)

        @pl.when(i > 0)
        def _():
            pass_plane(z)

        fetch(z)
        return carry

    def one_score(i, carry):
        z = lax.rem(t.z + i, t.nz)
        wait_bytes(side(z, 1 - t.c), q_sib.at[z])
        score(z)
        return carry

    lax.fori_loop(0, t.nz, one_fetch, 0)
    lax.fori_loop(0, t.nz, one_score, 0)

    column_rows = t.nz * r8
    send(ps.at[span(1 - t.c, t.flat * column_rows)], s1, s_send.at[0], s_recv.at[0], sibling)
    wait_bytes(s1, s_recv.at[0])

    def score_part(y, x):
        number = y * t.nx + x
        return (ps[span(t.c * t.flat + number, column_rows), :] + s1[span(number, column_rows), :])

    for o, y, x in t.plane():
        s2out[o] = score_part(y, x)
        send(s2out.at[o], s2.at[o], s_send.at[o], s_recv.at[o], t.device(t.z, t.c, y, x))
    total = score_part(t.y, t.x)
    for o, _ in around:
        wait_bytes(s2.at[o], s_recv.at[o])
        total = total + s2[o]
    s2out[0] = total
    for i, device in column:
        send(s2out.at[0, span((t.z + i) % t.nz, r8)], s3.at[i], s_send.at[t.flat + i], s_recv.at[t.flat + i], device)
    scores = s2out[0, span(t.z, r8), :]
    for i, _ in column:
        wait_bytes(s3.at[i], s_recv.at[t.flat + i])
        scores = scores + s3[i]

    log_retriever = log_normalize(scores * scale, k)
    weights = (jnp.exp(log_retriever) - reader_prob).astype(bf16).astype(f32)
    both = 2 * r8
    mall[span(t.mine, both), :] = jnp.concatenate(
        [weights, reader_prob * (log_reader - log_retriever)], axis=0)
    share_z(mall, both, w_sems)
    share_plane(mall, both, w_sems)
    share_sibling(mall, both, w_sems)
    share_done(mall, both, w_sems)

    at_row = iota((rows, r8 * LANES), 1)
    pick = (iota((rows, r8 * LANES), 0) == at_row % LANES // k * r8 + at_row // LANES).astype(f32).astype(bf16)

    def grads(i):
        z = lax.rem(t.z + i, t.nz)

        def one_sub(u, carry):
            for v in range(SUB):
                position = z * t.chunk + u * SUB + v
                small = (u * SUB + v) * t.nz + z
                spot = rank[span(small, r8), :]
                w = mall[pl.ds(pl.multiple_of(small * 2 * r8, 2 * r8), r8), :]
                spread = jnp.concatenate(
                    [jnp.where(slots == spot[b:b + 1, :], w[b:b + 1, :], 0.0).astype(bf16) for b in range(r8)],
                    axis=1)
                by_slot = lax.dot_general(
                    pick, spread, (((1,), (1,)), ((), ())), preferred_element_type=f32).astype(bf16)
                g[i, pl.ds(pl.multiple_of((u * SUB + v) * rows, rows), rows), :] = jnp.dot(
                    by_slot, held[pl.ds(pl.multiple_of(position * cap, cap), cap), :],
                    preferred_element_type=f32)
            return carry

        lax.fori_loop(0, t.chunk // SUB, one_sub, 0)
        first(i).start()

    def first(i):
        return pltpu.make_async_remote_copy(
            src_ref=g.at[i, span(1 - t.c, half)], dst_ref=sib.at[i],
            send_sem=sib_send.at[i], recv_sem=sib_recv.at[i],
            device_id=sibling, device_id_type=MESH)

    def second(i, o, y, x):
        return pltpu.make_async_remote_copy(
            src_ref=going.at[i, o], dst_ref=coming.at[i, o],
            send_sem=p_send.at[i, o], recv_sem=p_recv.at[i, o],
            device_id=t.device(t.z, t.c, y, x), device_id_type=MESH)

    def third(i):
        return pltpu.make_async_remote_copy(
            src_ref=acc.at[i], dst_ref=zin.at[i],
            send_sem=z_send.at[i], recv_sem=z_recv.at[i],
            device_id=t.device(lax.rem(t.z + i, t.nz), t.c, t.y, t.x), device_id_type=MESH)

    def summed(i, y, x):
        number = y * t.nx + x
        return (g[i, pl.ds(pl.multiple_of(t.c * half + number * rows, rows), rows), :]
                + sib[i, span(number, rows), :])

    def in_plane(i):
        first(i).wait_recv()
        for o, y, x in t.plane():
            going[i, o] = summed(i, y, x).astype(bf16)
            second(i, o, y, x).start()
        acc[i] = summed(i, t.y, t.x)

    def along_z(i):
        total = acc[i]
        for o, y, x in t.plane():
            second(i, o, y, x).wait_recv()
            total = total + coming[i, o].astype(f32)
        acc[i] = total

    def turn(step):
        return lax.rem(step + 1, t.nz)

    def one_step(step, carry):
        grads(turn(step))

        @pl.when(step >= 1)
        def _():
            in_plane(turn(step - 1))

        @pl.when(step >= 2)
        def _():
            along_z(turn(step - 2))
            third(turn(step - 2)).start()

        return carry

    lax.fori_loop(0, t.nz, one_step, 0)
    in_plane(0)
    along_z(t.nz - 1)
    third(t.nz - 1).start()
    divergence = mall[...].reshape(t.n, 2 * r8, LANES)[:, r8:, :]
    mean[0, 0] = jnp.sum(jnp.sum(divergence, axis=0)) / (t.n * rows)
    along_z(0)
    total = acc[0]
    for i in range(1, t.nz):
        third(i).wait_recv()
        total = total + zin[i]
    out[...] = total

    wait_bytes(qall.at[pl.ds(0, (t.n - 1) * rows)], q_send)
    wait_bytes(idall.at[pl.ds(0, (t.n - 1) * r8)], id_sems[0])
    wait_bytes(mall.at[pl.ds(0, (t.n - 1) * both)], w_sems[0])
    wait_bytes(s1, s_send.at[0])
    for o, _ in around:
        wait_bytes(s2.at[o], s_send.at[o])
    for i, _ in column:
        wait_bytes(s3.at[i], s_send.at[t.flat + i])
    for i in range(t.nz):
        first(i).wait_send()
        for o, y, x in t.plane():
            second(i, o, y, x).wait_send()
        if i:
            third(i).wait_send()


def solution(mesh):
    n_index, n_bulk = mesh.shape["index"], mesh.shape["bulk"]
    ny = n_index // 2
    nx = math.gcd(ny, n_bulk)
    nz = n_bulk // nx
    flat = ny * nx
    n = n_index * n_bulk
    vmem = pl.BlockSpec(memory_space=pltpu.VMEM)
    dma = pltpu.SemaphoreType.DMA

    def body(questions, passages, candidate_ids, reader_loglik):
        rows, k = candidate_ids.shape
        per, width = passages.shape
        r8 = rows * k // LANES
        scale = 4.0 / math.sqrt(width)
        f32, bf16, i32 = jnp.float32, jnp.bfloat16, jnp.int32
        cap = 2 * rows * k // n
        grads, mean = pl.pallas_call(
            functools.partial(kernel, (ny, nz, nx), scale, cap),
            out_shape=(jax.ShapeDtypeStruct((rows, width), f32), jax.ShapeDtypeStruct((1, 1), f32)),
            in_specs=[pl.BlockSpec(memory_space=pl.ANY)] * 4,
            out_specs=(vmem, pl.BlockSpec(memory_space=pltpu.SMEM)),
            scratch_shapes=[
                pltpu.VMEM((per, width), bf16),
                pltpu.VMEM((rows, k), i32),
                pltpu.VMEM((rows, k), f32),
                pltpu.VMEM((n * rows, width), bf16),
                pltpu.VMEM((n * r8, LANES), i32),
                pltpu.VMEM((n * r8, LANES), f32),
                pltpu.VMEM((SUB * cap, per), bf16),
                pltpu.VMEM((n * cap + LANES, width), bf16),
                pltpu.VMEM((n * r8, LANES), f32),
                pltpu.VMEM((n // 2 * r8, LANES), f32),
                pltpu.VMEM((flat, nz * r8, LANES), f32),
                pltpu.VMEM((flat, nz * r8, LANES), f32),
                pltpu.VMEM((nz, r8, LANES), f32),
                pltpu.VMEM((n * 2 * r8, LANES), f32),
                pltpu.VMEM((nz, 2 * flat * rows, width), f32),
                pltpu.VMEM((nz, flat * rows, width), f32),
                pltpu.VMEM((nz, rows, width), f32),
                pltpu.VMEM((nz, flat, rows, width), bf16),
                pltpu.VMEM((nz, flat, rows, width), bf16),
                pltpu.VMEM((nz, rows, width), f32),
                dma, dma((3,)), dma, dma((n,)), dma((nz,)), dma, dma((nz,)), dma((flat,)), dma,
                dma((flat + nz,)), dma((flat + nz,)), dma, dma((nz,)), dma((flat,)), dma,
                dma((nz,)), dma((nz,)), dma((nz, flat)), dma((nz, flat)), dma((nz,)), dma((nz,)),
            ],
            compiler_params=pltpu.CompilerParams(
                collective_id=0, has_side_effects=True, vmem_limit_bytes=VMEM_LIMIT),
            name="retriever_step",
        )(questions, passages, candidate_ids, reader_loglik)
        return mean[0, 0], grads * scale

    placed = P(("index", "bulk"), None)
    return jax.shard_map(
        body, mesh=mesh, in_specs=(placed,) * 4, out_specs=(P(), placed), check_vma=False)
```

```python
import functools
import math

import jax
import jax.numpy as jnp
from jax import lax
from jax.experimental import pallas as pl
from jax.experimental.pallas import tpu as pltpu
from jax.sharding import PartitionSpec as P

MESH = pl.DeviceIdType.MESH
LANES = 128
SUB = 8
VMEM_LIMIT = 58 * 1024 * 1024


class Place:
    def __init__(self, sizes):
        self.ny, self.nz, self.nx = sizes
        self.flat = self.ny * self.nx
        self.chunk = 2 * self.flat
        self.n = self.chunk * self.nz
        index, bulk = lax.axis_index("index"), lax.axis_index("bulk")
        self.y, self.c = index // 2, index % 2
        self.z, self.x = bulk // self.nx, bulk % self.nx
        self.me = self.position(self.z, self.c, self.y, self.x)
        self.owner = index * self.nz * self.nx + bulk

    def position(self, z, c, y, x):
        return (z * 2 + c) * self.flat + y * self.nx + x

    def device(self, z, c, y, x):
        return (y * 2 + c, z * self.nx + x)

    def others(self, act):
        def one_plane(i, carry):
            z = lax.rem(self.z + i, self.nz)
            for c in (self.c, 1 - self.c):
                for a in range(self.ny):
                    for b in range(self.nx):
                        y, x = lax.rem(self.y + a, self.ny), lax.rem(self.x + b, self.nx)
                        if c is self.c and a == 0 and b == 0:
                            @pl.when(i > 0)
                            def _():
                                act(self.device(z, c, y, x))
                        else:
                            act(self.device(z, c, y, x))
            return carry

        lax.fori_loop(0, self.nz, one_plane, 0)

    def plane(self):
        for a in range(self.ny):
            for b in range(self.nx):
                if a or b:
                    yield (a * self.nx + b, (self.y + a) % self.ny, (self.x + b) % self.nx)


def wait_bytes(ref, sem):
    pltpu.make_async_copy(ref, ref, sem).wait()


def grouped(x, k, reduce, empty):
    group = lax.broadcasted_iota(jnp.int32, x.shape, 1) // k
    result = jnp.full(x.shape, empty, x.dtype)
    for j in range(x.shape[1] // k):
        value = reduce(jnp.where(group == j, x, empty), axis=1, keepdims=True)
        result = jnp.where(group == j, value, result)
    return result


def log_normalize(x, k):
    shifted = x - grouped(x, k, jnp.max, -jnp.inf)
    return shifted - jnp.log(grouped(jnp.exp(shifted), k, jnp.sum, 0.0))


def kernel(sizes, scale, cap, q_hbm, p_hbm, id_hbm, reader_hbm, out, mean,
           p_ref, id_ref, reader_ref, qall, idall, rank, s, found, held, ps, srecv, mine, mall, g, sib, acc, going, coming, zout, zin,
           p_sem, in_sem, q_send, q_recv, id_send, id_recv, s_send, s_recv, w_send, w_recv,
           sib_send, sib_recv, p_send, p_recv, z_send, z_recv):
    t = Place(sizes)
    rows, k = id_ref.shape
    per, width = p_ref.shape
    tiles, group = per // LANES, LANES // k
    r8 = rows // group
    half = t.flat * rows
    f32, bf16 = jnp.float32, jnp.bfloat16

    def span(number, count):
        return pl.ds(pl.multiple_of(number * count, count), count)

    mine_in = [
        pltpu.make_async_copy(id_hbm, id_ref, in_sem.at[0]),
        pltpu.make_async_copy(reader_hbm, reader_ref, in_sem.at[1]),
        pltpu.make_async_copy(q_hbm, qall.at[span(t.me, rows)], in_sem.at[2]),
    ]
    for copy in mine_in:
        copy.start()
    load = pltpu.make_async_copy(p_hbm, p_ref, p_sem)
    load.start()
    barrier = pltpu.get_barrier_semaphore()

    t.others(lambda device: pl.semaphore_signal(
        barrier, inc=1, device_id=device, device_id_type=MESH))

    def packed(ref):
        return jnp.concatenate([ref[j * r8:(j + 1) * r8, :] for j in range(group)], axis=1)

    for copy in mine_in:
        copy.wait()
    idall[span(t.me, r8), :] = packed(id_ref)
    log_reader = log_normalize(packed(reader_ref), k)
    reader_prob = jnp.exp(log_reader)
    pl.semaphore_wait(barrier, t.n - 1)

    def to_all(src, dst, send_sem, recv_sem):
        t.others(lambda device: pltpu.make_async_remote_copy(
            src_ref=src, dst_ref=dst, send_sem=send_sem, recv_sem=recv_sem,
            device_id=device, device_id_type=MESH).start())

    def block(position):
        return qall.at[span(position, rows)]

    def give(src, position, device):
        pltpu.make_async_remote_copy(
            src_ref=src, dst_ref=block(position), send_sem=q_send, recv_sem=q_recv.at[position],
            device_id=device, device_id_type=MESH,
        ).start()

    def arrived(position):
        wait_bytes(block(position), q_recv.at[position])

    sibling = t.device(t.z, 1 - t.c, t.y, t.x)
    for i in range(1, t.nz):
        give(block(t.me), t.me, t.device((t.z + i) % t.nz, t.c, t.y, t.x))
    for _, y, x in t.plane():
        give(block(t.me), t.me, t.device(t.z, t.c, y, x))
    give(block(t.me), t.me, sibling)
    to_all(idall.at[span(t.me, r8)], idall.at[span(t.me, r8)], id_send, id_recv)

    for i in range(1, t.nz):
        position = t.position((t.z + i) % t.nz, t.c, t.y, t.x)
        arrived(position)
        for _, y, x in t.plane():
            give(block(position), position, t.device(t.z, t.c, y, x))
        give(block(position), position, sibling)

    def pass_plane(z):
        for _, y, x in t.plane():
            position = t.position(z, t.c, y, x)
            arrived(position)
            give(block(position), position, sibling)

    wait_bytes(idall.at[pl.ds(0, (t.n - 1) * r8)], id_recv)

    def iota(shape, dim):
        return lax.broadcasted_iota(jnp.int32, shape, dim)

    lane_group = iota((r8, LANES), 1) // k
    slots = iota((cap, LANES), 0).astype(f32)
    lanes = iota((cap, LANES), 1).astype(f32)
    count = SUB * r8
    before = (iota((LANES, LANES), 0) < iota((LANES, LANES), 1)).astype(f32).astype(bf16)
    row, col = iota((count, count), 0), iota((count, count), 1)
    above = ((row // r8 == col // r8) & (col < row)).astype(f32).astype(bf16)

    def one_rank(u, carry):
        at = pl.ds(pl.multiple_of(u * count, count), count)
        local = idall[at, :] - t.owner * per
        own = (local >= 0) & (local < per)
        ones = own.astype(f32).astype(bf16)
        earlier = jnp.dot(ones, before, preferred_element_type=f32)
        rows_above = jnp.sum(jnp.dot(above, ones, preferred_element_type=f32), axis=1, keepdims=True)
        rank[at, :] = jnp.where(own, earlier + rows_above, -1.0)
        return carry

    lax.fori_loop(0, t.n // SUB, one_rank, 0)
    load.wait()
    held[t.n * cap:, :] = jnp.zeros((LANES, width), bf16)

    def fetch(z):
        def one_sub(u, carry):
            first = z * t.chunk + u * SUB
            for v in range(SUB):
                at = span(first + v, r8)
                spot = rank[at, :]
                value = (idall[at, :] - t.owner * per + 1).astype(f32)
                chosen = jnp.zeros((cap, LANES), f32)
                for b in range(r8):
                    chosen = jnp.where(slots == spot[b:b + 1, :], value[b:b + 1, :], chosen)
                wanted = jnp.sum(chosen, axis=1, keepdims=True) - 1.0
                wanted = jnp.broadcast_to(wanted, (cap, LANES))
                high = jnp.floor(wanted * (1.0 / LANES))
                low_hot = jnp.where(lanes == wanted - high * LANES, 1.0, 0.0).astype(bf16)
                high = high.astype(bf16)
                for h in range(tiles):
                    found[v * cap:(v + 1) * cap, h * LANES:(h + 1) * LANES] = jnp.where(
                        high == jnp.full((cap, LANES), h, bf16), low_hot, jnp.zeros_like(low_hot))
            held[pl.ds(pl.multiple_of(first * cap, SUB * cap), SUB * cap), :] = jnp.dot(
                found[...], p_ref[...], preferred_element_type=f32).astype(bf16)
            return carry

        lax.fori_loop(0, t.chunk // SUB, one_sub, 0)

    def score(z):
        def one_sub(u, carry):
            first = z * t.chunk + u * SUB
            q = qall[pl.ds(pl.multiple_of(first * rows, SUB * rows), SUB * rows), :]
            codes, lows, totals = [], [], [None] * SUB
            for i in range(SUB):
                local = idall[span(first + i, r8), :] - t.owner * per
                own = (local >= 0) & (local < per)
                codes.append(jnp.where(own, lane_group * tiles + local // LANES, -1))
                lows.append(local & (LANES - 1))
            for h in range(0, tiles, 2):
                s[h // 2] = lax.dot_general(
                    q, p_ref[h * LANES:(h + 2) * LANES, :],
                    (((1,), (1,)), ((), ())), preferred_element_type=f32)
            for h in range(tiles):
                for i in range(SUB):
                    for j in range(group):
                        piece = s[h // 2, i * rows + j * r8:i * rows + (j + 1) * r8,
                                  h % 2 * LANES:(h % 2 + 1) * LANES]
                        picked = jnp.take_along_axis(piece, lows[i], axis=1)
                        picked = jnp.where(codes[i] == j * tiles + h, picked, 0.0)
                        totals[i] = picked if totals[i] is None else totals[i] + picked
            for i in range(SUB):
                ps[span(first + i, r8), :] = totals[i]
            return carry

        lax.fori_loop(0, t.chunk // SUB, one_sub, 0)
        for c in range(2):
            for y in range(t.ny):
                for x in range(t.nx):
                    position = t.position(z, c, y, x)

                    @pl.when(position != t.me)
                    def _():
                        pltpu.make_async_remote_copy(
                            src_ref=ps.at[span(position, r8)], dst_ref=srecv.at[span(t.me, r8)],
                            send_sem=s_send, recv_sem=s_recv,
                            device_id=t.device(z, c, y, x), device_id_type=MESH,
                        ).start()

    def weigh():
        srecv[span(t.me, r8), :] = ps[span(t.me, r8), :]
        wait_bytes(srecv.at[pl.ds(0, (t.n - 1) * r8)], s_recv)
        scores = jnp.sum(srecv[...].reshape(t.n, r8, LANES), axis=0) * scale
        log_retriever = log_normalize(scores, k)
        weights = (jnp.exp(log_retriever) - reader_prob).astype(bf16).astype(f32)
        mine[0:r8, :] = weights
        mine[r8:2 * r8, :] = reader_prob * (log_reader - log_retriever)
        to_all(mine, mall.at[span(t.me, 2 * r8)], w_send, w_recv.at[t.z])
        mall[span(t.me, 2 * r8), :] = mine[...]

    pass_plane(t.z)
    fetch(t.z)

    def one_plane(i, carry):
        @pl.when(i + 1 < t.nz)
        def _():
            pass_plane(lax.rem(t.z + i + 1, t.nz))

        z = lax.rem(t.z + i, t.nz)
        arrived(t.position(z, 1 - t.c, t.y, t.x))
        for _, y, x in t.plane():
            arrived(t.position(z, 1 - t.c, y, x))
        score(z)
        return carry

    lax.fori_loop(0, t.nz, one_plane, 0)

    def one_fetch(i, carry):
        fetch(lax.rem(t.z + i, t.nz))

        @pl.when(i == 1)
        def _():
            weigh()

        return carry

    lax.fori_loop(1, t.nz, one_fetch, 0)

    at_row = iota((rows, r8 * LANES), 1)
    pick = (iota((rows, r8 * LANES), 0) == at_row % LANES // k * r8 + at_row // LANES).astype(f32).astype(bf16)

    def grads(i):
        z = lax.rem(t.z + i, t.nz)
        weights_of = lambda count: wait_bytes(
            mall.at[pl.ds(pl.multiple_of(z * t.chunk * 2 * r8, 2 * r8), count * 2 * r8)], w_recv.at[z])

        @pl.when(i != 0)
        def _():
            weights_of(t.chunk)

        @pl.when(i == 0)
        def _():
            weights_of(t.chunk - 1)

        def one_sub(u, carry):
            for v in range(SUB):
                position = z * t.chunk + u * SUB + v
                spot = rank[span(position, r8), :]
                w = mall[pl.ds(pl.multiple_of(position * 2 * r8, 2 * r8), r8), :]
                spread = jnp.concatenate(
                    [jnp.where(slots == spot[b:b + 1, :], w[b:b + 1, :], 0.0).astype(bf16) for b in range(r8)],
                    axis=1)
                by_slot = lax.dot_general(
                    pick, spread, (((1,), (1,)), ((), ())), preferred_element_type=f32).astype(bf16)
                g[i, pl.ds(pl.multiple_of((u * SUB + v) * rows, rows), rows), :] = jnp.dot(
                    by_slot, held[pl.ds(pl.multiple_of(position * cap, cap), cap), :],
                    preferred_element_type=f32)
            return carry

        lax.fori_loop(0, t.chunk // SUB, one_sub, 0)
        first(i).start()

    def first(i):
        return pltpu.make_async_remote_copy(
            src_ref=g.at[i, span(1 - t.c, half)], dst_ref=sib.at[i],
            send_sem=sib_send.at[i], recv_sem=sib_recv.at[i],
            device_id=sibling, device_id_type=MESH)

    def second(i, o, y, x):
        return pltpu.make_async_remote_copy(
            src_ref=going.at[i, o], dst_ref=coming.at[i, o],
            send_sem=p_send.at[i, o], recv_sem=p_recv.at[i, o],
            device_id=t.device(t.z, t.c, y, x), device_id_type=MESH)

    def third(i):
        return pltpu.make_async_remote_copy(
            src_ref=zout.at[i], dst_ref=zin.at[i],
            send_sem=z_send.at[i], recv_sem=z_recv.at[i],
            device_id=t.device(lax.rem(t.z + i, t.nz), t.c, t.y, t.x), device_id_type=MESH)

    def summed(i, y, x):
        number = y * t.nx + x
        return (g[i, pl.ds(pl.multiple_of(t.c * half + number * rows, rows), rows), :]
                + sib[i, span(number, rows), :])

    def in_plane(i):
        first(i).wait_recv()
        for o, y, x in t.plane():
            going[i, o] = summed(i, y, x).astype(bf16)
            second(i, o, y, x).start()
        acc[i] = summed(i, t.y, t.x)

    def along_z(i):
        total = acc[i]
        for o, y, x in t.plane():
            second(i, o, y, x).wait_recv()
            total = total + coming[i, o].astype(f32)
        acc[i] = total
        zout[i] = total.astype(bf16)

    def turn(step):
        return lax.rem(step + 1, t.nz)

    def one_step(step, carry):
        grads(turn(step))

        @pl.when(step >= 1)
        def _():
            in_plane(turn(step - 1))

        @pl.when(step >= 2)
        def _():
            along_z(turn(step - 2))
            third(turn(step - 2)).start()

        return carry

    lax.fori_loop(0, t.nz, one_step, 0)
    in_plane(0)
    along_z(t.nz - 1)
    third(t.nz - 1).start()
    divergence = mall[...].reshape(t.n, 2 * r8, LANES)[:, r8:, :]
    mean[0, 0] = jnp.sum(jnp.sum(divergence, axis=0)) / (t.n * rows)
    along_z(0)
    total = acc[0]
    for i in range(1, t.nz):
        third(i).wait_recv()
        total = total + zin[i].astype(f32)
    out[...] = total

    wait_bytes(qall.at[pl.ds(0, (t.n - 1) * rows)], q_send)
    wait_bytes(idall.at[pl.ds(0, (t.n - 1) * r8)], id_send)
    wait_bytes(srecv.at[pl.ds(0, (t.n - 1) * r8)], s_send)
    wait_bytes(mall.at[pl.ds(0, (t.n - 1) * 2 * r8)], w_send)
    for i in range(t.nz):
        first(i).wait_send()
        for o, y, x in t.plane():
            second(i, o, y, x).wait_send()
        if i:
            third(i).wait_send()


def solution(mesh):
    n_index, n_bulk = mesh.shape["index"], mesh.shape["bulk"]
    ny = n_index // 2
    nx = math.gcd(ny, n_bulk)
    nz = n_bulk // nx
    flat = ny * nx
    n = n_index * n_bulk
    vmem = pl.BlockSpec(memory_space=pltpu.VMEM)
    dma = pltpu.SemaphoreType.DMA

    def body(questions, passages, candidate_ids, reader_loglik):
        rows, k = candidate_ids.shape
        per, width = passages.shape
        r8 = rows * k // LANES
        scale = 4.0 / math.sqrt(width)
        f32, bf16, i32 = jnp.float32, jnp.bfloat16, jnp.int32
        cap = 2 * rows * k // n
        grads, mean = pl.pallas_call(
            functools.partial(kernel, (ny, nz, nx), scale, cap),
            out_shape=(jax.ShapeDtypeStruct((rows, width), f32), jax.ShapeDtypeStruct((1, 1), f32)),
            in_specs=[pl.BlockSpec(memory_space=pl.ANY)] * 4,
            out_specs=(vmem, pl.BlockSpec(memory_space=pltpu.SMEM)),
            scratch_shapes=[
                pltpu.VMEM((per, width), bf16),
                pltpu.VMEM((rows, k), i32),
                pltpu.VMEM((rows, k), f32),
                pltpu.VMEM((n * rows, width), bf16),
                pltpu.VMEM((n * r8, LANES), i32),
                pltpu.VMEM((n * r8, LANES), f32),
                pltpu.VMEM((per // LANES // 2, SUB * rows, 2 * LANES), f32),
                pltpu.VMEM((SUB * cap, per), bf16),
                pltpu.VMEM((n * cap + LANES, width), bf16),
                pltpu.VMEM((n * r8, LANES), f32),
                pltpu.VMEM((n * r8, LANES), f32),
                pltpu.VMEM((2 * r8, LANES), f32),
                pltpu.VMEM((n * 2 * r8, LANES), f32),
                pltpu.VMEM((nz, 2 * flat * rows, width), f32),
                pltpu.VMEM((nz, flat * rows, width), f32),
                pltpu.VMEM((nz, rows, width), f32),
                pltpu.VMEM((nz, flat, rows, width), bf16),
                pltpu.VMEM((nz, flat, rows, width), bf16),
                pltpu.VMEM((nz, rows, width), bf16),
                pltpu.VMEM((nz, rows, width), bf16),
                dma, dma((3,)), dma, dma((n,)), dma, dma, dma, dma, dma, dma((nz,)),
                dma((nz,)), dma((nz,)), dma((nz, flat)), dma((nz, flat)), dma((nz,)), dma((nz,)),
            ],
            compiler_params=pltpu.CompilerParams(
                collective_id=0, has_side_effects=True, vmem_limit_bytes=VMEM_LIMIT),
            name="retriever_step",
        )(questions, passages, candidate_ids, reader_loglik)
        return mean[0, 0], grads * scale

    placed = P(("index", "bulk"), None)
    return jax.shard_map(
        body, mesh=mesh, in_specs=(placed,) * 4, out_specs=(P(), placed), check_vma=False)
```

```python
import functools
import math

import jax
import jax.numpy as jnp
from jax import lax
from jax.experimental import pallas as pl
from jax.experimental.pallas import tpu as pltpu
from jax.sharding import PartitionSpec as P

MESH = pl.DeviceIdType.MESH
LANES = 128
SUB = 8
VMEM_LIMIT = 58 * 1024 * 1024


class Place:
    def __init__(self, sizes):
        self.ny, self.nz, self.nx = sizes
        self.flat = self.ny * self.nx
        self.chunk = 2 * self.flat
        self.n = self.chunk * self.nz
        index, bulk = lax.axis_index("index"), lax.axis_index("bulk")
        self.y, self.c = index // 2, index % 2
        self.z, self.x = bulk // self.nx, bulk % self.nx
        self.me = self.position(self.z, self.c, self.y, self.x)
        self.owner = index * self.nz * self.nx + bulk

    def position(self, z, c, y, x):
        return (z * 2 + c) * self.flat + y * self.nx + x

    def device(self, z, c, y, x):
        return (y * 2 + c, z * self.nx + x)

    def others(self, act):
        def one_plane(i, carry):
            z = lax.rem(self.z + i, self.nz)
            for c in (self.c, 1 - self.c):
                for a in range(self.ny):
                    for b in range(self.nx):
                        y, x = lax.rem(self.y + a, self.ny), lax.rem(self.x + b, self.nx)
                        if c is self.c and a == 0 and b == 0:
                            @pl.when(i > 0)
                            def _():
                                act(self.device(z, c, y, x))
                        else:
                            act(self.device(z, c, y, x))
            return carry

        lax.fori_loop(0, self.nz, one_plane, 0)

    def plane(self):
        for a in range(self.ny):
            for b in range(self.nx):
                if a or b:
                    yield (a * self.nx + b, (self.y + a) % self.ny, (self.x + b) % self.nx)


def wait_bytes(ref, sem):
    pltpu.make_async_copy(ref, ref, sem).wait()


def grouped(x, k, reduce, empty):
    group = lax.broadcasted_iota(jnp.int32, x.shape, 1) // k
    result = jnp.full(x.shape, empty, x.dtype)
    for j in range(x.shape[1] // k):
        value = reduce(jnp.where(group == j, x, empty), axis=1, keepdims=True)
        result = jnp.where(group == j, value, result)
    return result


def log_normalize(x, k):
    shifted = x - grouped(x, k, jnp.max, -jnp.inf)
    return shifted - jnp.log(grouped(jnp.exp(shifted), k, jnp.sum, 0.0))


def kernel(sizes, scale, cap, q_hbm, p_hbm, id_hbm, reader_hbm, out, mean,
           p_ref, id_ref, reader_ref, qall, idall, rank, s, found, held, ps, srecv, mine, mall, g, sib, acc, going, coming, zout, zin,
           p_sem, in_sem, q_send, q_recv, id_send, id_recv, s_send, s_recv, w_send, w_recv,
           sib_send, sib_recv, p_send, p_recv, z_send, z_recv):
    t = Place(sizes)
    rows, k = id_ref.shape
    per, width = p_ref.shape
    tiles, group = per // LANES, LANES // k
    r8 = rows // group
    half = t.flat * rows
    f32, bf16 = jnp.float32, jnp.bfloat16

    def span(number, count):
        return pl.ds(pl.multiple_of(number * count, count), count)

    mine_in = [
        pltpu.make_async_copy(id_hbm, id_ref, in_sem.at[0]),
        pltpu.make_async_copy(reader_hbm, reader_ref, in_sem.at[1]),
        pltpu.make_async_copy(q_hbm, qall.at[span(t.me, rows)], in_sem.at[2]),
    ]
    for copy in mine_in:
        copy.start()
    load = pltpu.make_async_copy(p_hbm, p_ref, p_sem)
    load.start()
    barrier = pltpu.get_barrier_semaphore()

    t.others(lambda device: pl.semaphore_signal(
        barrier, inc=1, device_id=device, device_id_type=MESH))

    def packed(ref):
        return jnp.concatenate([ref[j * r8:(j + 1) * r8, :] for j in range(group)], axis=1)

    for copy in mine_in:
        copy.wait()
    idall[span(t.me, r8), :] = packed(id_ref)
    log_reader = log_normalize(packed(reader_ref), k)
    reader_prob = jnp.exp(log_reader)
    pl.semaphore_wait(barrier, t.n - 1)

    def to_all(src, dst, send_sem, recv_sem):
        t.others(lambda device: pltpu.make_async_remote_copy(
            src_ref=src, dst_ref=dst, send_sem=send_sem, recv_sem=recv_sem,
            device_id=device, device_id_type=MESH).start())

    def block(position):
        return qall.at[span(position, rows)]

    def give(src, position, device):
        pltpu.make_async_remote_copy(
            src_ref=src, dst_ref=block(position), send_sem=q_send, recv_sem=q_recv.at[position],
            device_id=device, device_id_type=MESH,
        ).start()

    def arrived(position):
        wait_bytes(block(position), q_recv.at[position])

    sibling = t.device(t.z, 1 - t.c, t.y, t.x)
    for i in range(1, t.nz):
        give(block(t.me), t.me, t.device((t.z + i) % t.nz, t.c, t.y, t.x))
    for _, y, x in t.plane():
        give(block(t.me), t.me, t.device(t.z, t.c, y, x))
    give(block(t.me), t.me, sibling)
    to_all(idall.at[span(t.me, r8)], idall.at[span(t.me, r8)], id_send, id_recv)

    for i in range(1, t.nz):
        position = t.position((t.z + i) % t.nz, t.c, t.y, t.x)
        arrived(position)
        for _, y, x in t.plane():
            give(block(position), position, t.device(t.z, t.c, y, x))
        give(block(position), position, sibling)

    def pass_plane(z):
        for _, y, x in t.plane():
            position = t.position(z, t.c, y, x)
            arrived(position)
            give(block(position), position, sibling)

    wait_bytes(idall.at[pl.ds(0, (t.n - 1) * r8)], id_recv)

    def iota(shape, dim):
        return lax.broadcasted_iota(jnp.int32, shape, dim)

    lane_group = iota((r8, LANES), 1) // k
    slots = iota((cap, LANES), 0).astype(f32)
    lanes = iota((cap, LANES), 1).astype(f32)
    count = SUB * r8
    before = (iota((LANES, LANES), 0) < iota((LANES, LANES), 1)).astype(f32).astype(bf16)
    row, col = iota((count, count), 0), iota((count, count), 1)
    above = ((row // r8 == col // r8) & (col < row)).astype(f32).astype(bf16)

    def one_rank(u, carry):
        at = pl.ds(pl.multiple_of(u * count, count), count)
        local = idall[at, :] - t.owner * per
        own = (local >= 0) & (local < per)
        ones = own.astype(f32).astype(bf16)
        earlier = jnp.dot(ones, before, preferred_element_type=f32)
        rows_above = jnp.sum(jnp.dot(above, ones, preferred_element_type=f32), axis=1, keepdims=True)
        rank[at, :] = jnp.where(own, earlier + rows_above, -1.0)
        return carry

    lax.fori_loop(0, t.n // SUB, one_rank, 0)
    load.wait()
    held[t.n * cap:, :] = jnp.zeros((LANES, width), bf16)

    def fetch(z):
        def one_sub(u, carry):
            find(z * t.chunk + u * SUB)
            hold(z * t.chunk + u * SUB)
            return carry

        lax.fori_loop(0, t.chunk // SUB, one_sub, 0)

    def find(first):
        for v in range(SUB):
            at = span(first + v, r8)
            spot = rank[at, :]
            value = (idall[at, :] - t.owner * per + 1).astype(f32)
            chosen = jnp.zeros((cap, LANES), f32)
            for b in range(r8):
                chosen = jnp.where(slots == spot[b:b + 1, :], value[b:b + 1, :], chosen)
            wanted = jnp.sum(chosen, axis=1, keepdims=True) - 1.0
            wanted = jnp.broadcast_to(wanted, (cap, LANES))
            high = jnp.floor(wanted * (1.0 / LANES))
            low_hot = jnp.where(lanes == wanted - high * LANES, 1.0, 0.0).astype(bf16)
            high = high.astype(bf16)
            for h in range(tiles):
                found[v * cap:(v + 1) * cap, h * LANES:(h + 1) * LANES] = jnp.where(
                    high == jnp.full((cap, LANES), h, bf16), low_hot, jnp.zeros_like(low_hot))

    def hold(first):
        held[pl.ds(pl.multiple_of(first * cap, SUB * cap), SUB * cap), :] = jnp.dot(
            found[...], p_ref[...], preferred_element_type=f32).astype(bf16)

    def score(z, fetching):
        def one_sub(u, carry):
            first = z * t.chunk + u * SUB
            q = qall[pl.ds(pl.multiple_of(first * rows, SUB * rows), SUB * rows), :]
            codes, lows, totals = [], [], [None] * SUB
            for i in range(SUB):
                local = idall[span(first + i, r8), :] - t.owner * per
                own = (local >= 0) & (local < per)
                codes.append(jnp.where(own, lane_group * tiles + local // LANES, -1))
                lows.append(local & (LANES - 1))
            for h in range(0, tiles, 2):
                s[h // 2] = lax.dot_general(
                    q, p_ref[h * LANES:(h + 2) * LANES, :],
                    (((1,), (1,)), ((), ())), preferred_element_type=f32)
            if fetching:
                find(first)
                hold(first)
            for h in range(tiles):
                for i in range(SUB):
                    for j in range(group):
                        piece = s[h // 2, i * rows + j * r8:i * rows + (j + 1) * r8,
                                  h % 2 * LANES:(h % 2 + 1) * LANES]
                        picked = jnp.take_along_axis(piece, lows[i], axis=1)
                        picked = jnp.where(codes[i] == j * tiles + h, picked, 0.0)
                        totals[i] = picked if totals[i] is None else totals[i] + picked
            for i in range(SUB):
                ps[span(first + i, r8), :] = totals[i]
            return carry

        lax.fori_loop(0, t.chunk // SUB, one_sub, 0)
        for c in range(2):
            for y in range(t.ny):
                for x in range(t.nx):
                    position = t.position(z, c, y, x)

                    @pl.when(position != t.me)
                    def _():
                        pltpu.make_async_remote_copy(
                            src_ref=ps.at[span(position, r8)], dst_ref=srecv.at[span(t.me, r8)],
                            send_sem=s_send, recv_sem=s_recv,
                            device_id=t.device(z, c, y, x), device_id_type=MESH,
                        ).start()

    def weigh():
        srecv[span(t.me, r8), :] = ps[span(t.me, r8), :]
        wait_bytes(srecv.at[pl.ds(0, (t.n - 1) * r8)], s_recv)
        scores = jnp.sum(srecv[...].reshape(t.n, r8, LANES), axis=0) * scale
        log_retriever = log_normalize(scores, k)
        weights = (jnp.exp(log_retriever) - reader_prob).astype(bf16).astype(f32)
        mine[0:r8, :] = weights
        mine[r8:2 * r8, :] = reader_prob * (log_reader - log_retriever)
        to_all(mine, mall.at[span(t.me, 2 * r8)], w_send, w_recv.at[t.z])
        mall[span(t.me, 2 * r8), :] = mine[...]

    pass_plane(t.z)
    fetch(t.z)

    def one_plane(i, carry):
        @pl.when(i + 1 < t.nz)
        def _():
            pass_plane(lax.rem(t.z + i + 1, t.nz))

        z = lax.rem(t.z + i, t.nz)
        arrived(t.position(z, 1 - t.c, t.y, t.x))
        for _, y, x in t.plane():
            arrived(t.position(z, 1 - t.c, y, x))

        @pl.when(i == 1)
        def _():
            score(z, True)

        @pl.when(i != 1)
        def _():
            score(z, False)

        return carry

    lax.fori_loop(0, t.nz, one_plane, 0)

    def one_fetch(i, carry):
        fetch(lax.rem(t.z + i, t.nz))

        @pl.when(i == 2)
        def _():
            weigh()

        return carry

    lax.fori_loop(2, t.nz, one_fetch, 0)

    at_row = iota((rows, r8 * LANES), 1)
    pick = (iota((rows, r8 * LANES), 0) == at_row % LANES // k * r8 + at_row // LANES).astype(f32).astype(bf16)

    def grads(i):
        z = lax.rem(t.z + i, t.nz)
        weights_of = lambda count: wait_bytes(
            mall.at[pl.ds(pl.multiple_of(z * t.chunk * 2 * r8, 2 * r8), count * 2 * r8)], w_recv.at[z])

        @pl.when(i != 0)
        def _():
            weights_of(t.chunk)

        @pl.when(i == 0)
        def _():
            weights_of(t.chunk - 1)

        def one_sub(u, carry):
            for v in range(SUB):
                position = z * t.chunk + u * SUB + v
                spot = rank[span(position, r8), :]
                w = mall[pl.ds(pl.multiple_of(position * 2 * r8, 2 * r8), r8), :]
                spread = jnp.concatenate(
                    [jnp.where(slots == spot[b:b + 1, :], w[b:b + 1, :], 0.0).astype(bf16) for b in range(r8)],
                    axis=1)
                by_slot = lax.dot_general(
                    pick, spread, (((1,), (1,)), ((), ())), preferred_element_type=f32).astype(bf16)
                g[i, pl.ds(pl.multiple_of((u * SUB + v) * rows, rows), rows), :] = jnp.dot(
                    by_slot, held[pl.ds(pl.multiple_of(position * cap, cap), cap), :],
                    preferred_element_type=f32)
            return carry

        lax.fori_loop(0, t.chunk // SUB, one_sub, 0)
        first(i).start()

    def first(i):
        return pltpu.make_async_remote_copy(
            src_ref=g.at[i, span(1 - t.c, half)], dst_ref=sib.at[i],
            send_sem=sib_send.at[i], recv_sem=sib_recv.at[i],
            device_id=sibling, device_id_type=MESH)

    def second(i, o, y, x):
        return pltpu.make_async_remote_copy(
            src_ref=going.at[i, o], dst_ref=coming.at[i, o],
            send_sem=p_send.at[i, o], recv_sem=p_recv.at[i, o],
            device_id=t.device(t.z, t.c, y, x), device_id_type=MESH)

    def third(i):
        return pltpu.make_async_remote_copy(
            src_ref=zout.at[i], dst_ref=zin.at[i],
            send_sem=z_send.at[i], recv_sem=z_recv.at[i],
            device_id=t.device(lax.rem(t.z + i, t.nz), t.c, t.y, t.x), device_id_type=MESH)

    def summed(i, y, x):
        number = y * t.nx + x
        return (g[i, pl.ds(pl.multiple_of(t.c * half + number * rows, rows), rows), :]
                + sib[i, span(number, rows), :])

    def in_plane(i):
        first(i).wait_recv()
        for o, y, x in t.plane():
            going[i, o] = summed(i, y, x).astype(bf16)
            second(i, o, y, x).start()
        acc[i] = summed(i, t.y, t.x)

    def along_z(i):
        total = acc[i]
        for o, y, x in t.plane():
            second(i, o, y, x).wait_recv()
            total = total + coming[i, o].astype(f32)
        acc[i] = total
        zout[i] = total.astype(bf16)

    def turn(step):
        return lax.rem(step + 1, t.nz)

    def one_step(step, carry):
        grads(turn(step))

        @pl.when(step >= 1)
        def _():
            in_plane(turn(step - 1))

        @pl.when(step >= 2)
        def _():
            along_z(turn(step - 2))
            third(turn(step - 2)).start()

        return carry

    lax.fori_loop(0, t.nz, one_step, 0)
    in_plane(0)
    along_z(t.nz - 1)
    third(t.nz - 1).start()
    divergence = mall[...].reshape(t.n, 2 * r8, LANES)[:, r8:, :]
    mean[0, 0] = jnp.sum(jnp.sum(divergence, axis=0)) / (t.n * rows)
    along_z(0)
    total = acc[0]
    for i in range(1, t.nz):
        third(i).wait_recv()
        total = total + zin[i].astype(f32)
    out[...] = total

    wait_bytes(qall.at[pl.ds(0, (t.n - 1) * rows)], q_send)
    wait_bytes(idall.at[pl.ds(0, (t.n - 1) * r8)], id_send)
    wait_bytes(srecv.at[pl.ds(0, (t.n - 1) * r8)], s_send)
    wait_bytes(mall.at[pl.ds(0, (t.n - 1) * 2 * r8)], w_send)
    for i in range(t.nz):
        first(i).wait_send()
        for o, y, x in t.plane():
            second(i, o, y, x).wait_send()
        if i:
            third(i).wait_send()


def solution(mesh):
    n_index, n_bulk = mesh.shape["index"], mesh.shape["bulk"]
    ny = n_index // 2
    nx = math.gcd(ny, n_bulk)
    nz = n_bulk // nx
    flat = ny * nx
    n = n_index * n_bulk
    vmem = pl.BlockSpec(memory_space=pltpu.VMEM)
    dma = pltpu.SemaphoreType.DMA

    def body(questions, passages, candidate_ids, reader_loglik):
        rows, k = candidate_ids.shape
        per, width = passages.shape
        r8 = rows * k // LANES
        scale = 4.0 / math.sqrt(width)
        f32, bf16, i32 = jnp.float32, jnp.bfloat16, jnp.int32
        cap = 2 * rows * k // n
        grads, mean = pl.pallas_call(
            functools.partial(kernel, (ny, nz, nx), scale, cap),
            out_shape=(jax.ShapeDtypeStruct((rows, width), f32), jax.ShapeDtypeStruct((1, 1), f32)),
            in_specs=[pl.BlockSpec(memory_space=pl.ANY)] * 4,
            out_specs=(vmem, pl.BlockSpec(memory_space=pltpu.SMEM)),
            scratch_shapes=[
                pltpu.VMEM((per, width), bf16),
                pltpu.VMEM((rows, k), i32),
                pltpu.VMEM((rows, k), f32),
                pltpu.VMEM((n * rows, width), bf16),
                pltpu.VMEM((n * r8, LANES), i32),
                pltpu.VMEM((n * r8, LANES), f32),
                pltpu.VMEM((per // LANES // 2, SUB * rows, 2 * LANES), f32),
                pltpu.VMEM((SUB * cap, per), bf16),
                pltpu.VMEM((n * cap + LANES, width), bf16),
                pltpu.VMEM((n * r8, LANES), f32),
                pltpu.VMEM((n * r8, LANES), f32),
                pltpu.VMEM((2 * r8, LANES), f32),
                pltpu.VMEM((n * 2 * r8, LANES), f32),
                pltpu.VMEM((nz, 2 * flat * rows, width), f32),
                pltpu.VMEM((nz, flat * rows, width), f32),
                pltpu.VMEM((nz, rows, width), f32),
                pltpu.VMEM((nz, flat, rows, width), bf16),
                pltpu.VMEM((nz, flat, rows, width), bf16),
                pltpu.VMEM((nz, rows, width), bf16),
                pltpu.VMEM((nz, rows, width), bf16),
                dma, dma((3,)), dma, dma((n,)), dma, dma, dma, dma, dma, dma((nz,)),
                dma((nz,)), dma((nz,)), dma((nz, flat)), dma((nz, flat)), dma((nz,)), dma((nz,)),
            ],
            compiler_params=pltpu.CompilerParams(
                collective_id=0, has_side_effects=True, vmem_limit_bytes=VMEM_LIMIT),
            name="retriever_step",
        )(questions, passages, candidate_ids, reader_loglik)
        return mean[0, 0], grads * scale

    placed = P(("index", "bulk"), None)
    return jax.shard_map(
        body, mesh=mesh, in_specs=(placed,) * 4, out_specs=(P(), placed), check_vma=False)
```
